512 devices in a mesh: gx: 16 (over z, core), gy: 4 (over x), gz: 8 (over y).
Axes of the slice: x: 4, y: 8, z: 8, core: 2. Of those that a mesh axis runs over, the one named last changes fastest.
Arguments:
- velocity: float32 [3, 128, 64, 1024], P(None, 'gx', 'gy', 'gz'), may hold values from -6 to 6
- displacement: float32 [3, 128, 64, 1024], P(None, 'gx', 'gy', 'gz'), may hold values from -1.25 to 1.25
- mass: float32 [128, 64, 1024], P('gx', 'gy', 'gz'), may hold values from 0.5 to 2
- stress: float32 [6, 128, 64, 1024], P(None, 'gx', 'gy', 'gz'), may hold values from -3 to 3
- plastic: float32 [128, 64, 1024], P('gx', 'gy', 'gz'), may hold values from 0 to 0.5
- yield_stress: float32 [128, 64, 1024], P('gx', 'gy', 'gz'), may hold values from 0.5 to 3
- facet_anchor: float32 [16, 4, 8, 8, 3, 128], P('gx', 'gy', 'gz'), may hold values from 0 to 4
- facet_nodes: int32 [16, 4, 8, 8, 4, 128], P('gx', 'gy', 'gz'), may hold values from 0 to 16383
- pair_source: int32 [16, 4, 8, 256], P('gx', 'gy', 'gz'), may hold values from 0 to 7
- pair_dest: int32 [16, 4, 8, 256, 1], P('gx', 'gy', 'gz'), may hold values from 0 to 127; in each aligned block of 256 rows (0 to 255, 256 to 511, ..., all dimensions but the last counted through in order) at most 4 rows name the same one
- pair_target: int32 [16, 4, 8, 256], P('gx', 'gy', 'gz'), may hold values from 0 to 7
Outputs:
- velocity_new: float32 [3, 128, 64, 1024], P(None, 'gx', 'gy', 'gz')
- displacement_new: float32 [3, 128, 64, 1024], P(None, 'gx', 'gy', 'gz')
- stress_new: float32 [6, 128, 64, 1024], P(None, 'gx', 'gy', 'gz')
- plastic_new: float32 [128, 64, 1024], P('gx', 'gy', 'gz')
The draws below stay inside these ranges and needn't reach their ends.
Inputs may be any that keep to these rules, and one draw needn't show every extreme that they name: `pair_dest`: within the pairs of one device, no partner index appears more than 4 times.
All inputs are finite; a program needn't handle non-finite values.
Results may differ from the reference program's by a relative error of at most 0.00022.
Values sent between devices are 32-bit elements; how exact they have to be, the bound alone decides.
No kernel may reach another device: no remote copies, remote signals or barrier semaphores. Data moves between devices by JAX's collectives and lax.ppermute only.
A program may use at most 64 MiB of HBM per device.

```python
import math
import jax
import jax.numpy as jnp
import numpy as np
from jax import lax

EX = 8
EY = 16
EZ = 128
NB = 8
PAIRS = 256
FACETS = 128
CAP = 4
NX = 128
NY = 64
NZ = 1024
N_GX = 16
N_GY = 4
N_GZ = 8


def plant(result, key, least, top_value):
    longest = result.shape.index(max(result.shape))
    spots = []
    for shift in (0, 1):
        where = [jax.random.randint(jax.random.fold_in(key, axis), (), 0, length) for axis, length in enumerate(result.shape)]
        where[longest] = (where[longest] + shift) % result.shape[longest]
        spots.append(tuple(where))
    return result.at[spots[0]].set(least).at[spots[1]].set(top_value)


def level_of(stream_key, shape, shards, smallest, high):
    def one(position, blocks):
        heights = jax.random.uniform(jax.random.fold_in(jax.random.fold_in(stream_key, 6), position), (blocks,), jnp.float32, smallest / len(shards), high / len(shards))
        return jnp.repeat(jnp.exp(heights), shape[position] // blocks).reshape((-1,) + (1,) * (len(shape) - position - 1))

    level = one(*shards[0])
    for cut in shards[1:]:
        level = level * one(*cut)
    return level


def shared_out(rng, own, number, rows, count, top, bound, lean):
    order = jax.random.permutation(rng, count)
    crowded, common = portions_of(count, rows * top, bound, lean, True), portions_of(count, rows * top, bound, lean, False)
    places = jnp.arange(count)

    def named(tallies, turn):
        used = int((tallies > 0).sum())
        fixed = max(1, used // 4)
        moved = fixed + (places - fixed + turn * (used - fixed)) % max(1, count - fixed)
        return jnp.zeros((count,), jnp.int32).at[order[jnp.where(places < fixed, places, moved)]].set(jnp.asarray(tallies, jnp.int32))

    tallies = jnp.where(number % 4 == 0, named(crowded, number // 4), named(common, number - number // 4 - 1))
    mixed = jax.random.permutation(jax.random.fold_in(own, 3), count)
    source_of, taker = mixed[0:count // 2 * 2:2], mixed[1:count // 2 * 2:2]
    margin = jnp.minimum(tallies[source_of] - 1, bound - tallies[taker]) // 2
    margin = jnp.where((source_of == order[0]) | (taker == order[0]) | (tallies[taker] == 0), 0, jnp.maximum(margin, 0))
    moved = jax.random.randint(jax.random.fold_in(own, 4), (count // 2,), 0, 1 << 20) % (margin + 1)
    tallies = tallies.at[source_of].add(-moved).at[taker].add(moved)
    members = jnp.searchsorted(jnp.cumsum(tallies), jnp.arange(rows * top), side="right").astype(jnp.int32)
    grid = members.reshape(top, rows).T
    grid = grid[jax.random.permutation(jax.random.fold_in(own, 1), rows)]
    turn = jax.random.randint(jax.random.fold_in(own, 2), (rows, 1), 0, top)
    return jnp.take_along_axis(grid, (jnp.arange(top)[None, :] + turn) % top, axis=1)


def portions_of(number_of, total, bound, lean, full):
    weights = [(1 << 20) // math.isqrt(rank ** lean) + 1 for rank in range(1, number_of + 1)]
    largest = bound if full else min(bound, max(-(-total // number_of), total * weights[0] // sum(weights)))
    least = 1 if total - largest >= number_of - 1 else 0
    holding, rest = [largest] + [least] * (number_of - 1), total - largest - least * (number_of - 1)
    while rest > 0:
        movable = [i for i in range(1, number_of) if holding[i] < largest] or [i for i in range(1, number_of) if holding[i] < bound]
        pool, left = sum([weights[i] for i in movable]), rest
        for i in movable:
            more = min(bound - holding[i], max(1, left * weights[i] // pool), rest)
            holding[i] = holding[i] + more
            rest = rest - more
    return np.array(holding)


def bell_draw(own_key, dims, scale, reach, cuts=(), kind=jnp.bfloat16):
    loudness = level_of(own_key, dims, cuts, -0.22, 0.18) if cuts else 1.0
    entries = jax.random.normal(own_key, dims, jnp.float32) * scale * loudness
    return jnp.minimum(jnp.maximum(entries, -reach), reach).astype(kind)


def setup_inputs(seed: int = 0) -> dict:
    streams_of = jax.random.split(jax.random.key(seed), 12)
    velocity = bell_draw(streams_of[0], (3, NX, NY, NZ), 1.0, 6.0, ((1, 16), (2, 4), (3, 8)), jnp.float32)
    displacement = bell_draw(streams_of[1], (3, NX, NY, NZ), 0.2, 1.25, ((1, 16), (2, 4), (3, 8)), jnp.float32)
    mass = jnp.clip(jnp.exp(math.log(2.0) - 1.3862944 * jax.random.uniform(streams_of[2], (NX, NY, NZ), jnp.float32) ** level_of(streams_of[2], (NX, NY, NZ), ((0, 16), (1, 4), (2, 8)), -0.2, 0.2)), 0.5, 2.0)
    stress = bell_draw(streams_of[3], (6, NX, NY, NZ), 0.5, 3.0, ((1, 16), (2, 4), (3, 8)), jnp.float32)
    plastic = jnp.clip(0.5 * jax.random.uniform(streams_of[4], (NX, NY, NZ), jnp.float32) ** level_of(streams_of[4], (NX, NY, NZ), ((0, 16), (1, 4), (2, 8)), -0.2, 0.2), 0.0, 0.5)
    yield_stress = jnp.clip(jnp.exp(math.log(3.0) - 1.7917595 * jax.random.uniform(streams_of[5], (NX, NY, NZ), jnp.float32) ** level_of(streams_of[5], (NX, NY, NZ), ((0, 16), (1, 4), (2, 8)), -0.2, 0.2)), 0.5, 3.0)
    facet_anchor = jnp.clip(4.0 * jax.random.uniform(streams_of[6], (N_GX, N_GY, N_GZ, NB, 3, FACETS), jnp.float32) ** level_of(streams_of[6], (N_GX, N_GY, N_GZ, NB, 3, FACETS), ((0, 16), (1, 4), (2, 8)), -0.2, 0.2), 0.0, 4.0)
    facet_nodes = plant(jax.random.randint(streams_of[7], (N_GX, N_GY, N_GZ, NB, 4, FACETS), 0, EX * EY * EZ), jax.random.fold_in(streams_of[7], 1), 0, (EX * EY * EZ) - 1).astype(jnp.int32)
    pair_source = plant(jax.random.randint(streams_of[8], (N_GX, N_GY, N_GZ, PAIRS), 0, NB), jax.random.fold_in(streams_of[8], 1), 0, NB - 1).astype(jnp.int32)
    pair_dest_keys = jax.random.split(jax.random.fold_in(streams_of[9], 1), N_GX * N_GY * N_GZ * PAIRS // PAIRS)
    pair_dest_turns = jax.random.permutation(jax.random.fold_in(streams_of[9], 3), N_GX * N_GY * N_GZ * PAIRS // PAIRS)
    pair_dest = jax.vmap(lambda own, number: shared_out(jax.random.fold_in(streams_of[9], 2), own, number, PAIRS, N_GX * N_GZ, 1, CAP, 2))(pair_dest_keys, pair_dest_turns).reshape((N_GX, N_GY, N_GZ, PAIRS, 1))
    pair_target = plant(jax.random.randint(streams_of[10], (N_GX, N_GY, N_GZ, PAIRS), 0, NB), jax.random.fold_in(streams_of[10], 1), 0, NB - 1).astype(jnp.int32)
    return {"velocity": velocity, "displacement": displacement, "mass": mass, "stress": stress, "plastic": plastic, "yield_stress": yield_stress, "facet_anchor": facet_anchor, "facet_nodes": facet_nodes, "pair_source": pair_source, "pair_dest": pair_dest, "pair_target": pair_target}


TIME_STEP = 0.25
SHEAR_MODULUS = 1.0
BULK_MODULUS = 2.0
HARDENING = 1.0
PENALTY = 1.0
REACH_SQUARED = 1.0
CORNERS = ((0, 0, 0), (0, 0, 1), (0, 1, 0), (0, 1, 1), (1, 0, 0), (1, 0, 1), (1, 1, 0), (1, 1, 1))
VOIGT = ((0, 3, 5), (3, 1, 4), (5, 4, 2))

def velocity_gradient(corner_velocity):
    grad_rows = []
    for component in range(3):
        grad_row = []
        for direction in range(3):
            summed = 0.0
            for corner, corner_values in zip(CORNERS, corner_velocity):
                summed = summed + (2.0 * corner[direction] - 1.0) * corner_values[component]
            grad_row.append(0.25 * summed)
        grad_rows.append(grad_row)
    return grad_rows

def radial_return(grad, stress, plastic, yield_stress):
    inc_normal = [TIME_STEP * grad[axis_id][axis_id] for axis_id in range(3)]
    inc_shear = [TIME_STEP * 0.5 * (grad[0][1] + grad[1][0]), TIME_STEP * 0.5 * (grad[1][2] + grad[2][1]), TIME_STEP * 0.5 * (grad[0][2] + grad[2][0])]
    volume_inc = inc_normal[0] + inc_normal[1] + inc_normal[2]
    trial_normal = [stress[axis_id] + 2.0 * SHEAR_MODULUS * (inc_normal[axis_id] - volume_inc / 3.0) + BULK_MODULUS * volume_inc for axis_id in range(3)]
    trial_shear = [stress[3 + axis_id] + 2.0 * SHEAR_MODULUS * inc_shear[axis_id] for axis_id in range(3)]
    mean_stress = (trial_normal[0] + trial_normal[1] + trial_normal[2]) / 3.0
    dev_normal = [trial_normal[axis_id] - mean_stress for axis_id in range(3)]
    square_sum = dev_normal[0] * dev_normal[0] + dev_normal[1] * dev_normal[1] + dev_normal[2] * dev_normal[2]
    square_sum = square_sum + 2.0 * (trial_shear[0] * trial_shear[0] + trial_shear[1] * trial_shear[1] + trial_shear[2] * trial_shear[2])
    equivalent = jnp.sqrt(1.5 * square_sum)
    limit = yield_stress + HARDENING * plastic
    gamma = jnp.maximum(equivalent - limit, 0.0) / (3.0 * SHEAR_MODULUS + HARDENING)
    factor = 1.0 - 3.0 * SHEAR_MODULUS * gamma / jnp.maximum(equivalent, limit)
    components = [dev_normal[axis_id] * factor + mean_stress for axis_id in range(3)]
    components = components + [trial_shear[axis_id] * factor for axis_id in range(3)]
    return (jnp.stack(components), plastic + gamma)

def corner_force(stress_new, corner):
    forces = []
    for component in range(3):
        summed = 0.0
        for direction in range(3):
            summed = summed + stress_new[VOIGT[component][direction]] * (2.0 * corner[direction] - 1.0)
        forces.append(0.25 * summed)
    return jnp.stack(forces)

def contact_force(own_centroids, source_centroids):
    offset_vec = own_centroids[:, :, :, None] - source_centroids[:, :, None, :]
    distance_sq = lax.optimization_barrier(jnp.sum(offset_vec * offset_vec, axis=1))
    weight = PENALTY * jnp.maximum(REACH_SQUARED - distance_sq, 0.0)
    return lax.optimization_barrier(jnp.sum(weight[:, None, :, :] * offset_vec, axis=3))

def reference(velocity, displacement, mass, stress, plastic, yield_stress, facet_anchor, facet_nodes, pair_source, pair_dest, pair_target):
    padded = jnp.pad(velocity, ((0, 0), (0, 1), (0, 1), (0, 1)))
    corner_velocity = [padded[:, corner[0]:corner[0] + NX, corner[1]:corner[1] + NY, corner[2]:corner[2] + NZ] for corner in CORNERS]
    grad = velocity_gradient(corner_velocity)
    stress_new, plastic_new = radial_return(grad, stress, plastic, yield_stress)
    internal = jnp.zeros((3, NX + 1, NY + 1, NZ + 1), jnp.float32)
    for corner in CORNERS:
        internal = internal.at[:, corner[0]:corner[0] + NX, corner[1]:corner[1] + NY, corner[2]:corner[2] + NZ].add(corner_force(stress_new, corner))
    internal = internal[:, :NX, :NY, :NZ]
    devices = N_GX * N_GY * N_GZ
    node_total = EX * EY * EZ
    blocked = displacement.reshape(3, N_GX, EX, N_GY, EY, N_GZ, EZ).transpose(1, 3, 5, 0, 2, 4, 6).reshape(devices, 3, node_total)
    node_ids = facet_nodes.reshape(devices, NB, 4, FACETS)
    anchors = facet_anchor.reshape(devices, NB, 3, FACETS)

    def centroid_of(disp, ids, anchor):
        picked = disp[:, ids]
        return anchor + 0.25 * jnp.transpose(lax.optimization_barrier(jnp.sum(picked, axis=2)), (1, 0, 2))
    centroids = jax.vmap(centroid_of)(blocked, node_ids, anchors)
    flat_cent = centroids.reshape(devices * NB, 3, FACETS)
    source_dev = jnp.arange(devices, dtype=jnp.int32)
    layer_index = source_dev // N_GZ % N_GY
    dest_peer = pair_dest.reshape(devices, PAIRS).astype(jnp.int32)
    dest_dev = (dest_peer // N_GZ * N_GY + layer_index[:, None]) * N_GZ + dest_peer % N_GZ
    src_rows = (source_dev[:, None] * NB + pair_source.reshape(devices, PAIRS)).reshape(-1, 32)
    dst_rows = (dest_dev * NB + pair_target.reshape(devices, PAIRS)).reshape(-1, 32)

    def pair_forces(rows_pair):
        return contact_force(flat_cent[rows_pair[1]], flat_cent[rows_pair[0]])
    forces = lax.map(pair_forces, (src_rows, dst_rows))
    facet_force = jax.ops.segment_sum(forces.reshape(-1, 3, FACETS), dst_rows.reshape(-1), num_segments=devices * NB)
    facet_force = facet_force.reshape(devices, NB, 3, FACETS)

    def spread(ids, block_force):
        quarter_force = 0.25 * jnp.transpose(block_force, (1, 0, 2))
        node_force = jnp.zeros((3, node_total), jnp.float32)
        for corner_slot in range(4):
            node_force = node_force.at[:, ids[:, corner_slot, :]].add(quarter_force)
        return node_force
    contact = jax.vmap(spread)(node_ids, facet_force)
    contact = contact.reshape(N_GX, N_GY, N_GZ, 3, EX, EY, EZ).transpose(3, 0, 4, 1, 5, 2, 6).reshape(3, NX, NY, NZ)
    velocity_new = velocity + TIME_STEP * (contact - internal) / mass
    displacement_new = displacement + TIME_STEP * velocity_new
    return (velocity_new, displacement_new, stress_new, plastic_new)
```

```python
import jax
import jax.numpy as jnp
from jax import lax
from jax.experimental import pallas as pl
from jax.experimental.pallas import tpu as pltpu
from jax.sharding import PartitionSpec as P

FACETS = 128
SLOTS = 4
ROWS = 13
TIME_STEP = 0.25
SHEAR_MODULUS = 1.0
BULK_MODULUS = 2.0
HARDENING = 1.0
PENALTY = 1.0
REACH_SQUARED = 1.0
VOIGT = ((0, 3, 5), (3, 1, 4), (5, 4, 2))
NT = (((1,), (1,)), ((), ()))
VMEM = pl.BlockSpec(memory_space=pltpu.VMEM)
SMEM = pl.BlockSpec(memory_space=pltpu.SMEM)


def params(mib):
    return pltpu.CompilerParams(vmem_limit_bytes=mib * 1024 * 1024)


def split_2(value):
    high = value.astype(jnp.bfloat16)
    rest = (value - high.astype(jnp.float32)).astype(jnp.bfloat16)
    return high, rest


def lane_pick(value, lane):
    pick = (lax.broadcasted_iota(jnp.int32, (8, 128), 1) == lane).astype(jnp.float32)
    return lax.dot_general(
        pick, value, NT, precision=lax.Precision.HIGHEST, preferred_element_type=jnp.float32
    )[0:1]


def columns_of(rows):
    count = rows.shape[0]
    padded = jnp.concatenate([rows, jnp.zeros((128 - count, 128), jnp.float32)], axis=0)
    return padded.T


def low_z_kernel(velocity_ref, face_ref):
    face_ref[...] = lane_pick(velocity_ref[...], 0)


def pack_kernel(
    disp_ref, anchor_ref, nodes_ref, source_ref, dest_ref, target_ref, cent_ref, send_ref, count, slot_target
):
    peers = send_ref.shape[0] // ROWS
    pairs = source_ref.shape[0]
    high, rest = split_2(disp_ref[...])
    table = jnp.concatenate([high, rest], axis=1)
    iota = lax.broadcasted_iota(jnp.int32, (128, 4 * FACETS), 0)
    for block in range(anchor_ref.shape[0] // 3):
        ids = jnp.concatenate([nodes_ref[block * 4 + m : block * 4 + m + 1, :] for m in range(4)], axis=1)
        here = jnp.where(iota == (ids & 127), 1.0, 0.0).astype(jnp.bfloat16)
        picked = jnp.dot(table, jnp.concatenate([here, here], axis=0), preferred_element_type=jnp.float32)
        in_row = iota == (ids >> 7)
        for c in range(3):
            kept = jnp.where(in_row, picked[c * 128 : (c + 1) * 128], 0.0)
            total = kept[:, :128] + kept[:, 128:256] + kept[:, 256:384] + kept[:, 384:]
            total = jnp.sum(total, axis=0, keepdims=True)
            cent_ref[block * 3 + c] = anchor_ref[block * 3 + c] + 0.25 * total
    send_ref[...] = jnp.zeros(send_ref.shape, jnp.float32)

    def clear(peer, carry):
        count[peer] = 0
        for k in range(SLOTS):
            slot_target[peer * SLOTS + k] = -1
        return carry

    lax.fori_loop(0, peers, clear, 0)

    def place(pair, carry):
        dest = dest_ref[pair]
        slot = count[dest]
        count[dest] = slot + 1
        slot_target[dest * SLOTS + slot] = target_ref[pair]
        send_ref[pl.ds(dest * ROWS + 3 * slot, 3)] = cent_ref[pl.ds(source_ref[pair] * 3, 3)]
        return carry

    lax.fori_loop(0, pairs, place, 0, unroll=8)
    lane = lax.broadcasted_iota(jnp.int32, (1, 128), 1)

    def write_targets(peer, carry):
        row = jnp.full((1, 128), -1, jnp.int32)
        for k in range(SLOTS):
            row = jnp.where(lane == k, slot_target[peer * SLOTS + k], row)
        send_ref[peer * ROWS + ROWS - 1] = row.astype(jnp.float32)
        return carry

    lax.fori_loop(0, peers, write_targets, 0, unroll=4)


def spread_kernel(cent_ref, wide_ref):
    for r in range(wide_ref.shape[0]):
        wide_ref[r] = jnp.broadcast_to(cent_ref[r], (FACETS, FACETS)).T


def stress_kernel(
    velocity_ref, face_z_ref, face_x_ref, face_y_ref, stress_ref, plastic_ref, yield_ref,
    stress_out, plastic_out, upper_out, lower_out, edge_y_out, edge_x_out,
):
    nx = velocity_ref.shape[1]
    columns = columns_of(
        jnp.concatenate([face_z_ref[...], face_x_ref[48:51, :], face_y_ref[27:33, :]], axis=0)
    )
    lane = lax.broadcasted_iota(jnp.int32, (16, 128), 1)
    row = lax.broadcasted_iota(jnp.int32, (16, 128), 0)
    grad_x, grad_y, grad_z = ([], [], [])
    for c in range(3):
        sum_yz, dif_y, dif_z = ([], [], [])
        for x in range(nx + 1):
            if x < nx:
                plane = velocity_ref[c, x]
                beyond = columns[x * 16 : x * 16 + 16, c : c + 1]
                edge = face_y_ref[c * 8 + x : c * 8 + x + 1, :]
                edge_beyond = columns[x * 16 : x * 16 + 1, 6 + c : 7 + c]
            else:
                plane = face_x_ref[c * 16 : c * 16 + 16, :]
                beyond = columns[0:16, 3 + c : 4 + c]
                edge = face_y_ref[24 + c : 25 + c, :]
                edge_beyond = columns[0:1, 9 + c : 10 + c]
            edge = jnp.broadcast_to(edge, (16, 128))
            after = jnp.where(lane == 127, beyond, pltpu.roll(plane, 127, 1))
            edge_after = jnp.where(lane == 127, edge_beyond, pltpu.roll(edge, 127, 1))
            sum_z, dif = plane + after, after - plane
            sum_z_next = jnp.where(row == 15, edge + edge_after, pltpu.roll(sum_z, 15, 0))
            dif_next = jnp.where(row == 15, edge_after - edge, pltpu.roll(dif, 15, 0))
            sum_yz.append(sum_z + sum_z_next)
            dif_y.append(sum_z_next - sum_z)
            dif_z.append(dif + dif_next)
        grad_x.append([0.25 * (sum_yz[x + 1] - sum_yz[x]) for x in range(nx)])
        grad_y.append([0.25 * (dif_y[x + 1] + dif_y[x]) for x in range(nx)])
        grad_z.append([0.25 * (dif_z[x + 1] + dif_z[x]) for x in range(nx)])
    stresses = []
    for x in range(nx):
        inc = [TIME_STEP * grad_x[0][x], TIME_STEP * grad_y[1][x], TIME_STEP * grad_z[2][x]]
        shear = [
            TIME_STEP * 0.5 * (grad_y[0][x] + grad_x[1][x]),
            TIME_STEP * 0.5 * (grad_z[1][x] + grad_y[2][x]),
            TIME_STEP * 0.5 * (grad_z[0][x] + grad_x[2][x]),
        ]
        volume = inc[0] + inc[1] + inc[2]
        trial = [
            stress_ref[d, x] + 2.0 * SHEAR_MODULUS * (inc[d] - volume / 3.0) + BULK_MODULUS * volume
            for d in range(3)
        ]
        trial_shear = [stress_ref[3 + d, x] + 2.0 * SHEAR_MODULUS * shear[d] for d in range(3)]
        mean = (trial[0] + trial[1] + trial[2]) / 3.0
        dev = [trial[d] - mean for d in range(3)]
        square = dev[0] * dev[0] + dev[1] * dev[1] + dev[2] * dev[2]
        square = square + 2.0 * (
            trial_shear[0] * trial_shear[0] + trial_shear[1] * trial_shear[1] + trial_shear[2] * trial_shear[2]
        )
        equivalent = jnp.sqrt(1.5 * square)
        plastic = plastic_ref[x]
        limit = yield_ref[x] + HARDENING * plastic
        gamma = jnp.maximum(equivalent - limit, 0.0) / (3.0 * SHEAR_MODULUS + HARDENING)
        factor = 1.0 - 3.0 * SHEAR_MODULUS * gamma / jnp.maximum(equivalent, limit)
        new = [dev[d] * factor + mean for d in range(3)] + [trial_shear[d] * factor for d in range(3)]
        for d in range(6):
            stress_out[d, x] = new[d]
        plastic_out[x] = plastic + gamma
        stresses.append(new)
    for c in range(3):
        before = None
        edge_before = None
        for x in range(nx + 1):
            if x < nx:
                s = [0.25 * stresses[x][VOIGT[c][d]] for d in range(3)]
                down = [jnp.where(row == 0, 0.0, pltpu.roll(v, 1, 0)) for v in s]
                here = [down[0] + s[0], down[1] - s[1], down[2] + s[2]]
                edge_here = [v[15:16] for v in s]
            if x == 0:
                x0, x1, x2 = -here[0], here[1], here[2]
                e0, e1, e2 = -edge_here[0], edge_here[1], edge_here[2]
            elif x < nx:
                x0, x1, x2 = before[0] - here[0], before[1] + here[1], before[2] + here[2]
                e0, e1, e2 = (
                    edge_before[0] - edge_here[0], edge_before[1] + edge_here[1], edge_before[2] + edge_here[2]
                )
            else:
                x0, x1, x2 = before
                e0, e1, e2 = edge_before
            both = x0 + x1
            edge_both = e0 + e1
            if x < nx:
                upper_out[c, x] = both + x2
                lower_out[c, x] = both - x2
            else:
                edge_x_out[c] = both + x2
                edge_x_out[3 + c] = both - x2
            edge_y_out[c, x : x + 1, :] = edge_both + e2
            edge_y_out[3 + c, x : x + 1, :] = edge_both - e2
            before, edge_before = here, edge_here


def force_kernel(upper_ref, lower_ref, from_y_ref, from_x_ref, internal_out, face_out):
    nx = upper_ref.shape[1]
    lane = lax.broadcasted_iota(jnp.int32, (16, 128), 1)
    row = lax.broadcasted_iota(jnp.int32, (16, 128), 0)
    for c in range(3):
        planes = []
        for x in range(nx):
            upper = upper_ref[c, x] + jnp.where(row == 0, from_y_ref[c, x : x + 1, :], 0.0)
            lower = lower_ref[c, x] + jnp.where(row == 0, from_y_ref[3 + c, x : x + 1, :], 0.0)
            if x == 0:
                upper = upper + from_x_ref[c]
                lower = lower + from_x_ref[3 + c]
            planes.append(upper)
            internal_out[c, x] = lower + jnp.where(lane == 0, 0.0, pltpu.roll(upper, 1, 1))
        face_out[:, c * 128 : (c + 1) * 128] = lane_pick(jnp.concatenate(planes, axis=0), 127)


def pair_kernel(
    got_ref, got_rows_ref, wide_ref, nodes_ref, internal_ref, from_z_ref, velocity_ref, disp_ref, mass_ref,
    velocity_out, disp_out, targets, target_vec, sums, slots, count, semaphore,
):
    blocks = wide_ref.shape[0] // 3
    peers = got_ref.shape[0] // ROWS
    target_rows = got_rows_ref[pl.ds(ROWS - 1, peers, stride=ROWS), :]
    if peers < 128:
        target_rows = jnp.concatenate([target_rows, jnp.full((128 - peers, 128), -1.0)], axis=0)
    target_vec[...] = target_rows.T[0:8, :].astype(jnp.int32)
    copy = pltpu.make_async_copy(target_vec, targets, semaphore)
    copy.start()
    copy.wait()
    for block in range(blocks + 1):
        count[block] = 0
    room = SLOTS * peers

    def sort_peer(peer, carry):
        for k in range(SLOTS):
            target = targets[k, peer]
            block = jnp.where(target < 0, blocks, target)
            place = count[block]
            count[block] = place + 1
            slots[block * room + place] = peer * ROWS + 3 * k
        return carry

    lax.fori_loop(0, peers, sort_peer, 0, unroll=2)

    def one_block(block, carry):
        number = count[block]
        for start in range(0, FACETS, 32):
            own = [wide_ref[block * 3 + c, start : start + 32, :] for c in range(3)]

            def group(step, total):
                total = list(total)
                for k in range(4):
                    place = step * 4 + k
                    inside = place < number
                    base = slots[block * room + jnp.where(inside, place, 0)]
                    away = jnp.where(inside, 0.0, 1.0e4)
                    offset = [
                        own[0] - (got_ref[base] + away), own[1] - got_ref[base + 1], own[2] - got_ref[base + 2]
                    ]
                    distance = offset[0] * offset[0] + offset[1] * offset[1] + offset[2] * offset[2]
                    weight = PENALTY * jnp.maximum(REACH_SQUARED - distance, 0.0)
                    total = [total[c] + weight * offset[c] for c in range(3)]
                return tuple(total)

            zero = jnp.zeros((32, FACETS), jnp.float32)
            total = lax.fori_loop(0, (number + 3) >> 2, group, (zero, zero, zero))
            for c in range(3):
                sums[block * 3 + c, start : start + 32, :] = total[c]
        return carry

    lax.fori_loop(0, blocks, one_block, 0)
    ones = jnp.ones((8, FACETS), jnp.float32)
    iota = lax.broadcasted_iota(jnp.int32, (128, FACETS), 0)
    contact = jnp.zeros((384, 128), jnp.float32)
    for block in range(blocks):
        left, right = ([], [])
        parts = []
        for c in range(3):
            force = lax.dot_general(
                ones, sums[block * 3 + c], NT, precision=lax.Precision.HIGHEST, preferred_element_type=jnp.float32
            )[0:1]
            high, rest = split_2(0.25 * force)
            parts.append((high.astype(jnp.float32), rest.astype(jnp.float32)))
        for m in range(4):
            ids = nodes_ref[block * 4 + m : block * 4 + m + 1, :]
            here = jnp.where(iota == (ids & 127), 1.0, 0.0).astype(jnp.bfloat16)
            in_row = iota == (ids >> 7)
            for part in range(2):
                left.append(
                    jnp.concatenate(
                        [jnp.where(in_row, parts[c][part], 0.0).astype(jnp.bfloat16) for c in range(3)], axis=0
                    )
                )
                right.append(here)
        contact = contact + lax.dot_general(
            jnp.concatenate(left, axis=1), jnp.concatenate(right, axis=1), NT, preferred_element_type=jnp.float32
        )
    columns = columns_of(from_z_ref[...])
    lane = lax.broadcasted_iota(jnp.int32, (128, 128), 1)
    for c in range(3):
        rows = slice(c * 128, c * 128 + 128)
        internal = internal_ref[rows, :] + jnp.where(lane == 0, columns[:, c : c + 1], 0.0)
        velocity = velocity_ref[rows, :] + TIME_STEP * (contact[rows] - internal) / mass_ref[...]
        velocity_out[rows, :] = velocity
        disp_out[rows, :] = disp_ref[rows, :] + TIME_STEP * velocity


def shifted(value, axis, step):
    count = lax.axis_size(axis)
    return lax.ppermute(value, axis, [(i, i + step) for i in range(count) if 0 <= i + step < count])


def f32(*shape):
    return jax.ShapeDtypeStruct(shape, jnp.float32)


def on_device(
    velocity,
    displacement,
    mass,
    stress,
    plastic,
    yield_stress,
    facet_anchor,
    facet_nodes,
    pair_source,
    pair_dest,
    pair_target,
):
    size_x, size_y, size_z = velocity.shape[1:]
    blocks = facet_anchor.shape[3]
    pairs = pair_source.shape[3]
    peers = lax.axis_size("gx") * lax.axis_size("gz")
    flat_velocity = velocity.reshape(-1, size_z)
    flat_disp = displacement.reshape(-1, size_z)
    nodes = facet_nodes.reshape(blocks * 4, FACETS)
    anchors = facet_anchor.reshape(blocks * 3, 1, FACETS)

    low_z = pl.pallas_call(
        low_z_kernel, out_shape=f32(1, flat_velocity.shape[0]), compiler_params=params(8), name="low_z"
    )(flat_velocity)
    face_z = shifted(low_z, "gz", -1).reshape(3, 128)
    face_x = shifted(
        jnp.concatenate([velocity[:, 0].reshape(48, size_z), face_z], axis=0), "gx", -1
    )
    centroids, send = pl.pallas_call(
        pack_kernel,
        out_shape=(f32(blocks * 3, 1, FACETS), f32(peers * ROWS, 1, FACETS)),
        in_specs=[VMEM, VMEM, VMEM, SMEM, SMEM, SMEM],
        out_specs=(VMEM, VMEM),
        scratch_shapes=[pltpu.SMEM((peers,), jnp.int32), pltpu.SMEM((peers * SLOTS,), jnp.int32)],
        compiler_params=params(16),
        name="pack",
    )(
        flat_disp,
        anchors,
        nodes,
        pair_source.reshape(pairs),
        pair_dest.reshape(pairs),
        pair_target.reshape(pairs),
    )
    got = lax.all_to_all(send, ("gx", "gz"), split_axis=0, concat_axis=0, tiled=True)
    wide = pl.pallas_call(
        spread_kernel, out_shape=f32(blocks * 3, FACETS, FACETS), compiler_params=params(8), name="spread"
    )(centroids)
    face_y = shifted(
        jnp.concatenate(
            [
                velocity[:, :, 0].reshape(24, size_z),
                face_x[:48].reshape(3, 16, size_z)[:, 0],
                face_z,
                face_x[48:],
            ],
            axis=0,
        ),
        "gy",
        -1,
    )
    stress_new, plastic_new, upper, lower, edge_y, edge_x = pl.pallas_call(
        stress_kernel,
        out_shape=(
            f32(*stress.shape),
            f32(*plastic.shape),
            f32(*velocity.shape),
            f32(*velocity.shape),
            f32(6, size_x + 1, size_z),
            f32(6, size_y, size_z),
        ),
        compiler_params=params(16),
        name="stress",
    )(velocity, face_z, face_x, face_y, stress, plastic, yield_stress)
    from_y = shifted(edge_y, "gy", 1)
    from_x = shifted(edge_x.at[:, 0].add(from_y[:, size_x]), "gx", 1)
    internal, high_z = pl.pallas_call(
        force_kernel,
        out_shape=(f32(*velocity.shape), f32(1, flat_velocity.shape[0])),
        compiler_params=params(8),
        name="force",
    )(upper, lower, from_y, from_x)
    from_z = shifted(high_z, "gz", 1).reshape(3, 128)
    velocity_new, displacement_new = pl.pallas_call(
        pair_kernel,
        out_shape=(f32(*flat_velocity.shape), f32(*flat_velocity.shape)),
        scratch_shapes=[
            pltpu.SMEM((8, 128), jnp.int32),
            pltpu.VMEM((8, 128), jnp.int32),
            pltpu.VMEM((blocks * 3, FACETS, FACETS), jnp.float32),
            pltpu.SMEM(((blocks + 1) * SLOTS * peers,), jnp.int32),
            pltpu.SMEM((blocks + 1,), jnp.int32),
            pltpu.SemaphoreType.DMA,
        ],
        compiler_params=params(24),
        name="pairs",
    )(
        got,
        got.reshape(peers * ROWS, FACETS),
        wide,
        nodes,
        internal.reshape(-1, size_z),
        from_z,
        flat_velocity,
        flat_disp,
        mass.reshape(-1, size_z),
    )
    return (
        velocity_new.reshape(velocity.shape),
        displacement_new.reshape(velocity.shape),
        stress_new,
        plastic_new,
    )


def solution(mesh):
    return jax.shard_map(
        on_device,
        mesh=mesh,
        in_specs=(
            P(None, "gx", "gy", "gz"),
            P(None, "gx", "gy", "gz"),
            P("gx", "gy", "gz"),
            P(None, "gx", "gy", "gz"),
            P("gx", "gy", "gz"),
            P("gx", "gy", "gz"),
            P("gx", "gy", "gz", None, None, None),
            P("gx", "gy", "gz", None, None, None),
            P("gx", "gy", "gz", None),
            P("gx", "gy", "gz", None, None),
            P("gx", "gy", "gz", None),
        ),
        out_specs=(
            P(None, "gx", "gy", "gz"),
            P(None, "gx", "gy", "gz"),
            P(None, "gx", "gy", "gz"),
            P("gx", "gy", "gz"),
        ),
        check_vma=False,
    )
```

```python
import jax
import jax.numpy as jnp
from jax import lax
from jax.experimental import pallas as pl
from jax.experimental.pallas import tpu as pltpu
from jax.sharding import PartitionSpec as P

FACETS = 128
SLOTS = 4
CENTER = 2.0
GROUP = 4
ROWS = 13
TIME_STEP = 0.25
SHEAR_MODULUS = 1.0
BULK_MODULUS = 2.0
HARDENING = 1.0
PENALTY = 1.0
REACH_SQUARED = 1.0
VOIGT = ((0, 3, 5), (3, 1, 4), (5, 4, 2))
NT = (((1,), (1,)), ((), ()))
VMEM = pl.BlockSpec(memory_space=pltpu.VMEM)
HBM = pl.BlockSpec(memory_space=pltpu.HBM)


def params(mib):
    return pltpu.CompilerParams(vmem_limit_bytes=mib * 1024 * 1024)


def split_2(value):
    high = value.astype(jnp.bfloat16)
    rest = (value - high.astype(jnp.float32)).astype(jnp.bfloat16)
    return high, rest


def lane_pick(value, lane):
    pick = (lax.broadcasted_iota(jnp.int32, (8, 128), 1) == lane).astype(jnp.float32)
    return lax.dot_general(
        pick, value, NT, precision=lax.Precision.HIGHEST, preferred_element_type=jnp.float32
    )[0:1]


def columns_of(rows):
    count = rows.shape[0]
    padded = jnp.concatenate([rows, jnp.zeros((128 - count, 128), jnp.float32)], axis=0)
    return padded.T


def low_z_kernel(velocity_ref, face_ref):
    face_ref[...] = lane_pick(velocity_ref[...], 0)


def gather_kernel(disp_ref, anchor_ref, nodes_ref, cent_ref):
    high, rest = split_2(disp_ref[...])
    table = jnp.concatenate([high, rest], axis=1)
    iota = lax.broadcasted_iota(jnp.int32, (128, 4 * FACETS), 0)
    blocks = anchor_ref.shape[0] // 3
    for block in range(blocks):
        ids = jnp.concatenate([nodes_ref[block * 4 + m : block * 4 + m + 1, :] for m in range(4)], axis=1)
        here = jnp.where(iota == (ids & 127), 1.0, 0.0).astype(jnp.bfloat16)
        picked = jnp.dot(table, jnp.concatenate([here, here], axis=0), preferred_element_type=jnp.float32)
        in_row = iota == (ids >> 7)
        for c in range(3):
            kept = jnp.where(in_row, picked[c * 128 : (c + 1) * 128], 0.0)
            total = kept[:, :128] + kept[:, 128:256] + kept[:, 256:384] + kept[:, 384:]
            total = jnp.sum(total, axis=0, keepdims=True)
            cent_ref[block * 3 + c] = anchor_ref[c * blocks + block : c * blocks + block + 1, :] + 0.25 * total


def place_kernel(
    cent_ref, source_hbm, dest_hbm, target_hbm, send_ref, source_ref, dest_ref, target_ref, count, slot_target, sems
):
    peers = send_ref.shape[0] // ROWS
    pairs = source_ref.shape[0]
    copies = [
        pltpu.make_async_copy(source_hbm, source_ref, sems.at[0]),
        pltpu.make_async_copy(dest_hbm, dest_ref, sems.at[1]),
        pltpu.make_async_copy(target_hbm, target_ref, sems.at[2]),
    ]
    for copy in copies:
        copy.start()
    send_ref[...] = jnp.zeros(send_ref.shape, jnp.float32)

    def clear(peer, carry):
        count[peer] = 0
        for k in range(SLOTS):
            slot_target[peer * SLOTS + k] = -1
        return carry

    lax.fori_loop(0, peers, clear, 0, unroll=4)
    for copy in copies:
        copy.wait()

    def place(pair, carry):
        dest = dest_ref[pair]
        slot = count[dest]
        count[dest] = slot + 1
        slot_target[dest * SLOTS + slot] = target_ref[pair]
        send_ref[pl.ds(dest * ROWS + 3 * slot, 3)] = cent_ref[pl.ds(source_ref[pair] * 3, 3)]
        return carry

    lax.fori_loop(0, pairs, place, 0, unroll=8)
    lane = lax.broadcasted_iota(jnp.int32, (1, 128), 1)

    def write_targets(peer, carry):
        row = jnp.full((1, 128), -1, jnp.int32)
        for k in range(SLOTS):
            row = jnp.where(lane == k, slot_target[peer * SLOTS + k], row)
        send_ref[peer * ROWS + ROWS - 1] = row.astype(jnp.float32)
        return carry

    lax.fori_loop(0, peers, write_targets, 0, unroll=4)


def split_3(value):
    high = value.astype(jnp.bfloat16).astype(jnp.float32)
    rest = value - high
    middle = rest.astype(jnp.bfloat16).astype(jnp.float32)
    return high, middle, rest - middle


def own_kernel(cent_ref, own_ref):
    for block in range(own_ref.shape[0]):
        x, y, z = [cent_ref[block * 3 + c] - CENTER for c in range(3)]
        one = jnp.ones_like(x)
        rows = [2.0 * x, 2.0 * y, 2.0 * z, one, REACH_SQUARED - (x * x + y * y + z * z)]
        features = jnp.concatenate(rows + [jnp.zeros((3, FACETS), jnp.float32)], axis=0)
        high, middle, low = split_3(features)
        parts = jnp.concatenate([high, high, high, middle, middle, low, jnp.zeros((80, FACETS), jnp.float32)], axis=0)
        own_ref[block] = parts.T.astype(jnp.bfloat16)


def stress_kernel(
    velocity_ref, face_z_ref, face_x_ref, face_y_ref, stress_ref, plastic_ref, yield_ref,
    stress_out, plastic_out, upper_out, lower_out, edge_y_out, edge_x_out,
):
    nx = velocity_ref.shape[1]
    columns = columns_of(
        jnp.concatenate([face_z_ref[...], face_x_ref[48:51, :], face_y_ref[27:33, :]], axis=0)
    )
    lane = lax.broadcasted_iota(jnp.int32, (16, 128), 1)
    row = lax.broadcasted_iota(jnp.int32, (16, 128), 0)
    grad_x, grad_y, grad_z = ([], [], [])
    for c in range(3):
        sum_yz, dif_y, dif_z = ([], [], [])
        for x in range(nx + 1):
            if x < nx:
                plane = velocity_ref[c, x]
                beyond = columns[x * 16 : x * 16 + 16, c : c + 1]
                edge = face_y_ref[c * 8 + x : c * 8 + x + 1, :]
                edge_beyond = columns[x * 16 : x * 16 + 1, 6 + c : 7 + c]
            else:
                plane = face_x_ref[c * 16 : c * 16 + 16, :]
                beyond = columns[0:16, 3 + c : 4 + c]
                edge = face_y_ref[24 + c : 25 + c, :]
                edge_beyond = columns[0:1, 9 + c : 10 + c]
            edge = jnp.broadcast_to(edge, (16, 128))
            after = jnp.where(lane == 127, beyond, pltpu.roll(plane, 127, 1))
            edge_after = jnp.where(lane == 127, edge_beyond, pltpu.roll(edge, 127, 1))
            sum_z, dif = plane + after, after - plane
            sum_z_next = jnp.where(row == 15, edge + edge_after, pltpu.roll(sum_z, 15, 0))
            dif_next = jnp.where(row == 15, edge_after - edge, pltpu.roll(dif, 15, 0))
            sum_yz.append(sum_z + sum_z_next)
            dif_y.append(sum_z_next - sum_z)
            dif_z.append(dif + dif_next)
        grad_x.append([0.25 * (sum_yz[x + 1] - sum_yz[x]) for x in range(nx)])
        grad_y.append([0.25 * (dif_y[x + 1] + dif_y[x]) for x in range(nx)])
        grad_z.append([0.25 * (dif_z[x + 1] + dif_z[x]) for x in range(nx)])
    stresses = []
    for x in range(nx):
        inc = [TIME_STEP * grad_x[0][x], TIME_STEP * grad_y[1][x], TIME_STEP * grad_z[2][x]]
        shear = [
            TIME_STEP * 0.5 * (grad_y[0][x] + grad_x[1][x]),
            TIME_STEP * 0.5 * (grad_z[1][x] + grad_y[2][x]),
            TIME_STEP * 0.5 * (grad_z[0][x] + grad_x[2][x]),
        ]
        volume = inc[0] + inc[1] + inc[2]
        trial = [
            stress_ref[d, x] + 2.0 * SHEAR_MODULUS * (inc[d] - volume / 3.0) + BULK_MODULUS * volume
            for d in range(3)
        ]
        trial_shear = [stress_ref[3 + d, x] + 2.0 * SHEAR_MODULUS * shear[d] for d in range(3)]
        mean = (trial[0] + trial[1] + trial[2]) / 3.0
        dev = [trial[d] - mean for d in range(3)]
        square = dev[0] * dev[0] + dev[1] * dev[1] + dev[2] * dev[2]
        square = square + 2.0 * (
            trial_shear[0] * trial_shear[0] + trial_shear[1] * trial_shear[1] + trial_shear[2] * trial_shear[2]
        )
        equivalent = jnp.sqrt(1.5 * square)
        plastic = plastic_ref[x]
        limit = yield_ref[x] + HARDENING * plastic
        gamma = jnp.maximum(equivalent - limit, 0.0) / (3.0 * SHEAR_MODULUS + HARDENING)
        factor = 1.0 - 3.0 * SHEAR_MODULUS * gamma / jnp.maximum(equivalent, limit)
        new = [dev[d] * factor + mean for d in range(3)] + [trial_shear[d] * factor for d in range(3)]
        for d in range(6):
            stress_out[d, x] = new[d]
        plastic_out[x] = plastic + gamma
        stresses.append(new)
    for c in range(3):
        before = None
        edge_before = None
        for x in range(nx + 1):
            if x < nx:
                s = [0.25 * stresses[x][VOIGT[c][d]] for d in range(3)]
                down = [jnp.where(row == 0, 0.0, pltpu.roll(v, 1, 0)) for v in s]
                here = [down[0] + s[0], down[1] - s[1], down[2] + s[2]]
                edge_here = [v[15:16] for v in s]
            if x == 0:
                x0, x1, x2 = -here[0], here[1], here[2]
                e0, e1, e2 = -edge_here[0], edge_here[1], edge_here[2]
            elif x < nx:
                x0, x1, x2 = before[0] - here[0], before[1] + here[1], before[2] + here[2]
                e0, e1, e2 = (
                    edge_before[0] - edge_here[0], edge_before[1] + edge_here[1], edge_before[2] + edge_here[2]
                )
            else:
                x0, x1, x2 = before
                e0, e1, e2 = edge_before
            both = x0 + x1
            edge_both = e0 + e1
            if x < nx:
                upper_out[c, x] = both + x2
                lower_out[c, x] = both - x2
            else:
                edge_x_out[c] = both + x2
                edge_x_out[3 + c] = both - x2
            edge_y_out[c, x : x + 1, :] = edge_both + e2
            edge_y_out[3 + c, x : x + 1, :] = edge_both - e2
            before, edge_before = here, edge_here


def force_kernel(upper_ref, lower_ref, from_y_ref, from_x_ref, internal_out, face_out):
    nx = upper_ref.shape[1]
    lane = lax.broadcasted_iota(jnp.int32, (16, 128), 1)
    row = lax.broadcasted_iota(jnp.int32, (16, 128), 0)
    for c in range(3):
        planes = []
        for x in range(nx):
            upper = upper_ref[c, x] + jnp.where(row == 0, from_y_ref[c, x : x + 1, :], 0.0)
            lower = lower_ref[c, x] + jnp.where(row == 0, from_y_ref[3 + c, x : x + 1, :], 0.0)
            if x == 0:
                upper = upper + from_x_ref[c]
                lower = lower + from_x_ref[3 + c]
            planes.append(upper)
            internal_out[c, x] = lower + jnp.where(lane == 0, 0.0, pltpu.roll(upper, 1, 1))
        face_out[:, c * 128 : (c + 1) * 128] = lane_pick(jnp.concatenate(planes, axis=0), 127)


def pair_kernel(
    got_ref, got_rows_ref, own_ref, sums, targets, target_vec, slots, count, even, odd, semaphore
):
    blocks = own_ref.shape[0]
    peers = got_ref.shape[0] // ROWS
    target_rows = got_rows_ref[pl.ds(ROWS - 1, peers, stride=ROWS), :]
    if peers < 128:
        target_rows = jnp.concatenate([target_rows, jnp.full((128 - peers, 128), -1.0)], axis=0)
    target_vec[...] = target_rows.T[0:8, :].astype(jnp.int32)
    copy = pltpu.make_async_copy(target_vec, targets, semaphore)
    copy.start()
    copy.wait()
    for block in range(blocks + 1):
        count[block] = 0
    room = SLOTS * peers

    def sort_peer(peer, carry):
        for k in range(SLOTS):
            target = targets[k, peer]
            block = jnp.where(target < 0, blocks, target)
            place = count[block]
            count[block] = place + 1
            slots[block * room + place] = peer * ROWS + 3 * k
        return carry

    lax.fori_loop(0, peers, sort_peer, 0, unroll=2)
    sub = lax.broadcasted_iota(jnp.int32, (8, FACETS), 0)

    def one_block(block, carry):
        number = count[block]
        for q in range(4):
            sums[block * 4 + q] = jnp.zeros((FACETS, FACETS), jnp.float32)

        def base_of(place):
            inside = place < number
            return inside, jnp.where(inside, slots[block * room + jnp.where(inside, place, 0)], 0)

        def reach(step, out):
            columns = []
            for k in range(GROUP):
                inside, base = base_of(step * GROUP + k)
                x, y, z = [jnp.broadcast_to(got_ref[base + c], (8, FACETS)) - CENTER for c in range(3)]
                away = x * x + y * y + z * z + jnp.where(inside, 0.0, 1.0e6)
                value = jnp.where(sub == 4, 1.0, 0.0)
                for index, part in enumerate((x, y, z, -away)):
                    value = jnp.where(sub == index, part, value)
                high, middle, low = split_3(value)
                columns.append(jnp.concatenate([high, middle, low, high, middle, high], axis=0).astype(jnp.bfloat16))
            out[...] = jnp.dot(
                own_ref[block][:, :48], jnp.concatenate(columns, axis=1), preferred_element_type=jnp.float32
            )

        def add(step, near):
            rows = []
            for k in range(GROUP):
                base = base_of(step * GROUP + k)[1]
                rows.append([got_ref[base + c] - CENTER for c in range(3)])
            for start in range(0, FACETS, 32):
                part = slice(start, start + 32)
                total = [sums[block * 4 + q, part, :] for q in range(4)]
                for k in range(GROUP):
                    weight = PENALTY * jnp.maximum(near[part, k * FACETS : (k + 1) * FACETS], 0.0)
                    total[3] = total[3] + weight
                    for c in range(3):
                        total[c] = total[c] + weight * rows[k][c]
                for q in range(4):
                    sums[block * 4 + q, part, :] = total[q]

        reach(0, even)

        def two(step, carry):
            reach(2 * step + 1, odd)
            add(2 * step, even)
            reach(2 * step + 2, even)
            add(2 * step + 1, odd)
            return carry

        lax.fori_loop(0, (number + 2 * GROUP - 1) // (2 * GROUP), two, 0)
        return carry

    lax.fori_loop(0, blocks, one_block, 0)


def scatter_kernel(sums_ref, cent_ref, nodes_ref, contact_ref):
    blocks = cent_ref.shape[0] // 3
    ones = jnp.ones((8, FACETS), jnp.float32)
    iota = lax.broadcasted_iota(jnp.int32, (128, FACETS), 0)
    contact = jnp.zeros((384, 128), jnp.float32)
    for block in range(blocks):
        left, right = ([], [])
        total = [
            lax.dot_general(
                ones, sums_ref[block * 4 + q], NT, precision=lax.Precision.HIGHEST, preferred_element_type=jnp.float32
            )[0:1]
            for q in range(4)
        ]
        parts = []
        for c in range(3):
            force = (cent_ref[block * 3 + c] - CENTER) * total[3] - total[c]
            high, rest = split_2(0.25 * force)
            parts.append((high.astype(jnp.float32), rest.astype(jnp.float32)))
        for m in range(4):
            ids = nodes_ref[block * 4 + m : block * 4 + m + 1, :]
            here = jnp.where(iota == (ids & 127), 1.0, 0.0).astype(jnp.bfloat16)
            in_row = iota == (ids >> 7)
            for part in range(2):
                left.append(
                    jnp.concatenate(
                        [jnp.where(in_row, parts[c][part], 0.0).astype(jnp.bfloat16) for c in range(3)], axis=0
                    )
                )
                right.append(here)
        contact = contact + lax.dot_general(
            jnp.concatenate(left, axis=1), jnp.concatenate(right, axis=1), NT, preferred_element_type=jnp.float32
        )
    contact_ref[...] = contact


def update_kernel(
    contact_ref, internal_ref, from_z_ref, velocity_ref, disp_ref, mass_ref, velocity_out, disp_out
):
    columns = columns_of(from_z_ref[...])
    lane = lax.broadcasted_iota(jnp.int32, (128, 128), 1)
    for c in range(3):
        rows = slice(c * 128, c * 128 + 128)
        internal = internal_ref[rows, :] + jnp.where(lane == 0, columns[:, c : c + 1], 0.0)
        velocity = velocity_ref[rows, :] + TIME_STEP * (contact_ref[rows, :] - internal) / mass_ref[...]
        velocity_out[rows, :] = velocity
        disp_out[rows, :] = disp_ref[rows, :] + TIME_STEP * velocity


def shifted(value, axis, step):
    count = lax.axis_size(axis)
    return lax.ppermute(value, axis, [(i, i + step) for i in range(count) if 0 <= i + step < count])


def f32(*shape):
    return jax.ShapeDtypeStruct(shape, jnp.float32)


def on_device(
    velocity,
    displacement,
    mass,
    stress,
    plastic,
    yield_stress,
    facet_anchor,
    facet_nodes,
    pair_source,
    pair_dest,
    pair_target,
):
    size_x, size_y, size_z = velocity.shape[1:]
    blocks = facet_anchor.shape[3]
    pairs = pair_source.shape[3]
    peers = lax.axis_size("gx") * lax.axis_size("gz")
    flat_velocity = velocity.reshape(-1, size_z)
    flat_disp = displacement.reshape(-1, size_z)
    nodes = facet_nodes.reshape(blocks * 4, FACETS)
    anchors = facet_anchor.reshape(blocks, 3, FACETS).transpose(1, 0, 2).reshape(3 * blocks, FACETS)
    barrier = lax.optimization_barrier

    low_z = pl.pallas_call(
        low_z_kernel, out_shape=f32(1, flat_velocity.shape[0]), compiler_params=params(8), name="low_z"
    )(flat_velocity)
    face_z = shifted(low_z, "gz", -1)
    centroids = pl.pallas_call(
        gather_kernel, out_shape=f32(blocks * 3, 1, FACETS), compiler_params=params(16), name="gather"
    )(flat_disp, anchors, nodes)
    face_z, centroids = barrier((face_z, centroids))
    face_z = face_z.reshape(3, 128)
    face_x = shifted(
        jnp.concatenate([velocity[:, 0].reshape(48, size_z), face_z], axis=0), "gx", -1
    )
    send = pl.pallas_call(
        place_kernel,
        out_shape=f32(peers * ROWS, 1, FACETS),
        in_specs=[VMEM, HBM, HBM, HBM],
        out_specs=VMEM,
        scratch_shapes=[
            pltpu.SMEM((pairs,), jnp.int32),
            pltpu.SMEM((pairs,), jnp.int32),
            pltpu.SMEM((pairs,), jnp.int32),
            pltpu.SMEM((peers,), jnp.int32),
            pltpu.SMEM((peers * SLOTS,), jnp.int32),
            pltpu.SemaphoreType.DMA((3,)),
        ],
        compiler_params=params(16),
        name="place",
    )(centroids, pair_source.reshape(pairs), pair_dest.reshape(pairs), pair_target.reshape(pairs))
    face_y = shifted(
        jnp.concatenate(
            [
                velocity[:, :, 0].reshape(24, size_z),
                face_x[:48].reshape(3, 16, size_z)[:, 0],
                face_z,
                face_x[48:],
            ],
            axis=0,
        ),
        "gy",
        -1,
    )
    send, face_y, face_x = barrier((send, face_y, face_x))
    got = lax.all_to_all(send, ("gx", "gz"), split_axis=0, concat_axis=0, tiled=True)
    own = pl.pallas_call(
        own_kernel,
        out_shape=jax.ShapeDtypeStruct((blocks, FACETS, 128), jnp.bfloat16),
        compiler_params=params(8),
        name="own",
    )(centroids)
    stress_new, plastic_new, upper, lower, edge_y, edge_x = pl.pallas_call(
        stress_kernel,
        out_shape=(
            f32(*stress.shape),
            f32(*plastic.shape),
            f32(*velocity.shape),
            f32(*velocity.shape),
            f32(6, size_x + 1, size_z),
            f32(6, size_y, size_z),
        ),
        compiler_params=params(16),
        name="stress",
    )(velocity, face_z, face_x, face_y, stress, plastic, yield_stress)
    from_y = shifted(edge_y, "gy", 1)
    to_x = edge_x.at[:, 0].add(from_y[:, size_x])
    got, own, to_x = barrier((got, own, to_x))
    from_x = shifted(to_x, "gx", 1)
    sums = pl.pallas_call(
        pair_kernel,
        out_shape=f32(blocks * 4, FACETS, FACETS),
        scratch_shapes=[
            pltpu.SMEM((8, 128), jnp.int32),
            pltpu.VMEM((8, 128), jnp.int32),
            pltpu.SMEM(((blocks + 1) * SLOTS * peers,), jnp.int32),
            pltpu.SMEM((blocks + 1,), jnp.int32),
            pltpu.VMEM((FACETS, GROUP * FACETS), jnp.float32),
            pltpu.VMEM((FACETS, GROUP * FACETS), jnp.float32),
            pltpu.SemaphoreType.DMA,
        ],
        compiler_params=params(16),
        cost_estimate=pl.CostEstimate(flops=2 * 10**9, bytes_accessed=2**22, transcendentals=0),
        name="pairs",
    )(got, got.reshape(peers * ROWS, FACETS), own)
    from_x, sums = barrier((from_x, sums))
    internal, high_z = pl.pallas_call(
        force_kernel,
        out_shape=(f32(*velocity.shape), f32(1, flat_velocity.shape[0])),
        compiler_params=params(8),
        name="force",
    )(upper, lower, from_y, from_x)
    from_z = shifted(high_z, "gz", 1)
    contact = pl.pallas_call(
        scatter_kernel, out_shape=f32(384, 128), compiler_params=params(16), name="scatter"
    )(sums, centroids, nodes)
    from_z, contact = barrier((from_z, contact))
    velocity_new, displacement_new = pl.pallas_call(
        update_kernel,
        out_shape=(f32(*flat_velocity.shape), f32(*flat_velocity.shape)),
        compiler_params=params(8),
        name="update",
    )(
        contact,
        internal.reshape(-1, size_z),
        from_z.reshape(3, 128),
        flat_velocity,
        flat_disp,
        mass.reshape(-1, size_z),
    )
    return (
        velocity_new.reshape(velocity.shape),
        displacement_new.reshape(velocity.shape),
        stress_new,
        plastic_new,
    )


def solution(mesh):
    return jax.shard_map(
        on_device,
        mesh=mesh,
        in_specs=(
            P(None, "gx", "gy", "gz"),
            P(None, "gx", "gy", "gz"),
            P("gx", "gy", "gz"),
            P(None, "gx", "gy", "gz"),
            P("gx", "gy", "gz"),
            P("gx", "gy", "gz"),
            P("gx", "gy", "gz", None, None, None),
            P("gx", "gy", "gz", None, None, None),
            P("gx", "gy", "gz", None),
            P("gx", "gy", "gz", None, None),
            P("gx", "gy", "gz", None),
        ),
        out_specs=(
            P(None, "gx", "gy", "gz"),
            P(None, "gx", "gy", "gz"),
            P(None, "gx", "gy", "gz"),
            P("gx", "gy", "gz"),
        ),
        check_vma=False,
    )
```

```python
import jax
import jax.numpy as jnp
from jax import lax
from jax.experimental import pallas as pl
from jax.experimental.pallas import tpu as pltpu
from jax.sharding import PartitionSpec as P

FACETS = 128
SLOTS = 4
CENTER = 2.0
GROUP = 8
ROWS = 13
TIME_STEP = 0.25
SHEAR_MODULUS = 1.0
BULK_MODULUS = 2.0
HARDENING = 1.0
PENALTY = 1.0
REACH_SQUARED = 1.0
VOIGT = ((0, 3, 5), (3, 1, 4), (5, 4, 2))
NT = (((1,), (1,)), ((), ()))
VMEM = pl.BlockSpec(memory_space=pltpu.VMEM)
HBM = pl.BlockSpec(memory_space=pltpu.HBM)


def params(mib):
    return pltpu.CompilerParams(vmem_limit_bytes=mib * 1024 * 1024)


def split_2(value):
    high = value.astype(jnp.bfloat16)
    rest = (value - high.astype(jnp.float32)).astype(jnp.bfloat16)
    return high, rest


def lane_pick(value, lane):
    pick = (lax.broadcasted_iota(jnp.int32, (8, 128), 1) == lane).astype(jnp.float32)
    return lax.dot_general(
        pick, value, NT, precision=lax.Precision.HIGHEST, preferred_element_type=jnp.float32
    )[0:1]


def columns_of(rows):
    count = rows.shape[0]
    padded = jnp.concatenate([rows, jnp.zeros((128 - count, 128), jnp.float32)], axis=0)
    return padded.T


def rows_of(row):
    return [row[:, c * 128 : (c + 1) * 128] for c in range(row.shape[1] // 128)]


def faces_kernel(velocity_ref, low_z_ref, low_x_ref, low_y_ref):
    for c in range(3):
        planes = [velocity_ref[c, x] for x in range(velocity_ref.shape[1])]
        low_z_ref[:, c * 128 : (c + 1) * 128] = lane_pick(jnp.concatenate(planes, axis=0), 0)
        low_x_ref[c * 16 : (c + 1) * 16, :] = planes[0]
        low_y_ref[c * 8 : (c + 1) * 8, :] = jnp.concatenate([plane[0:1] for plane in planes], axis=0)


def edges_kernel(low_y_ref, face_x_ref, face_z_ref, face_xz_ref, out_ref):
    rows = [face_x_ref[c * 16 : c * 16 + 1, :] for c in range(3)]
    rows = rows + rows_of(face_z_ref[...]) + rows_of(face_xz_ref[...])
    out_ref[...] = jnp.concatenate([low_y_ref[...]] + rows + [jnp.zeros((7, 128), jnp.float32)], axis=0)


def gather_kernel(disp_ref, anchor_ref, nodes_ref, cent_ref):
    high, rest = split_2(disp_ref[...])
    table = jnp.concatenate([high, rest], axis=1)
    iota = lax.broadcasted_iota(jnp.int32, (128, 4 * FACETS), 0)
    blocks = anchor_ref.shape[0] // 3
    for block in range(blocks):
        ids = jnp.concatenate([nodes_ref[block * 4 + m : block * 4 + m + 1, :] for m in range(4)], axis=1)
        here = jnp.where(iota == (ids & 127), 1.0, 0.0).astype(jnp.bfloat16)
        picked = jnp.dot(table, jnp.concatenate([here, here], axis=0), preferred_element_type=jnp.float32)
        in_row = iota == (ids >> 7)
        for c in range(3):
            kept = jnp.where(in_row, picked[c * 128 : (c + 1) * 128], 0.0)
            total = kept[:, :128] + kept[:, 128:256] + kept[:, 256:384] + kept[:, 384:]
            total = jnp.sum(total, axis=0, keepdims=True)
            cent_ref[block * 3 + c] = anchor_ref[c * blocks + block : c * blocks + block + 1, :] + 0.25 * total


def place_kernel(
    cent_ref, source_hbm, dest_hbm, target_hbm, send_ref, source_ref, dest_ref, target_ref, count, slot_target, sems
):
    peers = send_ref.shape[0] // ROWS
    pairs = source_ref.shape[0]
    copies = [
        pltpu.make_async_copy(source_hbm, source_ref, sems.at[0]),
        pltpu.make_async_copy(dest_hbm, dest_ref, sems.at[1]),
        pltpu.make_async_copy(target_hbm, target_ref, sems.at[2]),
    ]
    for copy in copies:
        copy.start()
    def clear(peer, carry):
        count[peer] = 0
        for k in range(SLOTS):
            slot_target[peer * SLOTS + k] = -1
        return carry

    lax.fori_loop(0, peers, clear, 0, unroll=4)
    for copy in copies:
        copy.wait()

    def place(pair, carry):
        dest = dest_ref[pair]
        slot = count[dest]
        count[dest] = slot + 1
        slot_target[dest * SLOTS + slot] = target_ref[pair]
        send_ref[pl.ds(dest * ROWS + 3 * slot, 3)] = cent_ref[pl.ds(source_ref[pair] * 3, 3)]
        return carry

    lax.fori_loop(0, pairs, place, 0, unroll=8)
    lane = lax.broadcasted_iota(jnp.int32, (1, 128), 1)

    def write_targets(peer, carry):
        row = jnp.full((1, 128), -1, jnp.int32)
        for k in range(SLOTS):
            row = jnp.where(lane == k, slot_target[peer * SLOTS + k], row)
        send_ref[peer * ROWS + ROWS - 1] = row.astype(jnp.float32)
        return carry

    lax.fori_loop(0, peers, write_targets, 0, unroll=4)


def split_3(value):
    high = value.astype(jnp.bfloat16).astype(jnp.float32)
    rest = value - high
    middle = rest.astype(jnp.bfloat16).astype(jnp.float32)
    return high, middle, rest - middle


def own_kernel(cent_ref, own_ref):
    for block in range(own_ref.shape[0]):
        x, y, z = [cent_ref[block * 3 + c] - CENTER for c in range(3)]
        one = jnp.ones_like(x)
        rows = [2.0 * x, 2.0 * y, 2.0 * z, one, REACH_SQUARED - (x * x + y * y + z * z)]
        features = jnp.concatenate(rows + [jnp.zeros((3, FACETS), jnp.float32)], axis=0)
        high, middle, low = split_3(features)
        parts = jnp.concatenate([high, high, high, middle, middle, low, jnp.zeros((80, FACETS), jnp.float32)], axis=0)
        own_ref[block] = parts.T.astype(jnp.bfloat16)


def stress_kernel(
    velocity_ref, face_z_ref, face_x_ref, face_xz_ref, face_y_ref, stress_ref, plastic_ref, yield_ref,
    stress_out, plastic_out, upper_out, lower_out, edge_y_out, edge_x_out,
):
    nx = velocity_ref.shape[1]
    columns = columns_of(
        jnp.concatenate(rows_of(face_z_ref[...]) + rows_of(face_xz_ref[...]) + [face_y_ref[27:33, :]], axis=0)
    )
    lane = lax.broadcasted_iota(jnp.int32, (16, 128), 1)
    row = lax.broadcasted_iota(jnp.int32, (16, 128), 0)
    grad_x, grad_y, grad_z = ([], [], [])
    for c in range(3):
        sum_yz, dif_y, dif_z = ([], [], [])
        for x in range(nx + 1):
            if x < nx:
                plane = velocity_ref[c, x]
                beyond = columns[x * 16 : x * 16 + 16, c : c + 1]
                edge = face_y_ref[c * 8 + x : c * 8 + x + 1, :]
                edge_beyond = columns[x * 16 : x * 16 + 1, 6 + c : 7 + c]
            else:
                plane = face_x_ref[c * 16 : c * 16 + 16, :]
                beyond = columns[0:16, 3 + c : 4 + c]
                edge = face_y_ref[24 + c : 25 + c, :]
                edge_beyond = columns[0:1, 9 + c : 10 + c]
            edge = jnp.broadcast_to(edge, (16, 128))
            after = jnp.where(lane == 127, beyond, pltpu.roll(plane, 127, 1))
            edge_after = jnp.where(lane == 127, edge_beyond, pltpu.roll(edge, 127, 1))
            sum_z, dif = plane + after, after - plane
            sum_z_next = jnp.where(row == 15, edge + edge_after, pltpu.roll(sum_z, 15, 0))
            dif_next = jnp.where(row == 15, edge_after - edge, pltpu.roll(dif, 15, 0))
            sum_yz.append(sum_z + sum_z_next)
            dif_y.append(sum_z_next - sum_z)
            dif_z.append(dif + dif_next)
        grad_x.append([0.25 * (sum_yz[x + 1] - sum_yz[x]) for x in range(nx)])
        grad_y.append([0.25 * (dif_y[x + 1] + dif_y[x]) for x in range(nx)])
        grad_z.append([0.25 * (dif_z[x + 1] + dif_z[x]) for x in range(nx)])
    stresses = []
    for x in range(nx):
        inc = [TIME_STEP * grad_x[0][x], TIME_STEP * grad_y[1][x], TIME_STEP * grad_z[2][x]]
        shear = [
            TIME_STEP * 0.5 * (grad_y[0][x] + grad_x[1][x]),
            TIME_STEP * 0.5 * (grad_z[1][x] + grad_y[2][x]),
            TIME_STEP * 0.5 * (grad_z[0][x] + grad_x[2][x]),
        ]
        volume = inc[0] + inc[1] + inc[2]
        trial = [
            stress_ref[d, x] + 2.0 * SHEAR_MODULUS * (inc[d] - volume / 3.0) + BULK_MODULUS * volume
            for d in range(3)
        ]
        trial_shear = [stress_ref[3 + d, x] + 2.0 * SHEAR_MODULUS * shear[d] for d in range(3)]
        mean = (trial[0] + trial[1] + trial[2]) / 3.0
        dev = [trial[d] - mean for d in range(3)]
        square = dev[0] * dev[0] + dev[1] * dev[1] + dev[2] * dev[2]
        square = square + 2.0 * (
            trial_shear[0] * trial_shear[0] + trial_shear[1] * trial_shear[1] + trial_shear[2] * trial_shear[2]
        )
        equivalent = jnp.sqrt(1.5 * square)
        plastic = plastic_ref[x]
        limit = yield_ref[x] + HARDENING * plastic
        gamma = jnp.maximum(equivalent - limit, 0.0) / (3.0 * SHEAR_MODULUS + HARDENING)
        factor = 1.0 - 3.0 * SHEAR_MODULUS * gamma / jnp.maximum(equivalent, limit)
        new = [dev[d] * factor + mean for d in range(3)] + [trial_shear[d] * factor for d in range(3)]
        for d in range(6):
            stress_out[d, x] = new[d]
        plastic_out[x] = plastic + gamma
        stresses.append(new)
    for c in range(3):
        before = None
        edge_before = None
        for x in range(nx + 1):
            if x < nx:
                s = [0.25 * stresses[x][VOIGT[c][d]] for d in range(3)]
                down = [jnp.where(row == 0, 0.0, pltpu.roll(v, 1, 0)) for v in s]
                here = [down[0] + s[0], down[1] - s[1], down[2] + s[2]]
                edge_here = [v[15:16] for v in s]
            if x == 0:
                x0, x1, x2 = -here[0], here[1], here[2]
                e0, e1, e2 = -edge_here[0], edge_here[1], edge_here[2]
            elif x < nx:
                x0, x1, x2 = before[0] - here[0], before[1] + here[1], before[2] + here[2]
                e0, e1, e2 = (
                    edge_before[0] - edge_here[0], edge_before[1] + edge_here[1], edge_before[2] + edge_here[2]
                )
            else:
                x0, x1, x2 = before
                e0, e1, e2 = edge_before
            both = x0 + x1
            edge_both = e0 + e1
            if x < nx:
                upper_out[c, x] = both + x2
                lower_out[c, x] = both - x2
            else:
                edge_x_out[c] = both + x2
                edge_x_out[3 + c] = both - x2
            edge_y_out[c, x : x + 1, :] = edge_both + e2
            edge_y_out[3 + c, x : x + 1, :] = edge_both - e2
            before, edge_before = here, edge_here


def force_kernel(upper_ref, edge_x_ref, from_y_ref, to_x_ref, to_z_ref, to_xz_ref):
    nx = upper_ref.shape[1]
    row = lax.broadcasted_iota(jnp.int32, (16, 128), 0)

    def with_y(plane, c, x):
        return plane + jnp.where(row == 0, from_y_ref[c, x : x + 1, :], 0.0)

    corner = []
    for c in range(6):
        plane = with_y(edge_x_ref[c], c, nx)
        to_x_ref[c] = plane
        corner.append(plane)
    to_xz_ref[...] = lane_pick(jnp.concatenate(corner[:3] + [jnp.zeros((80, 128), jnp.float32)], axis=0), 127)
    for c in range(3):
        planes = [with_y(upper_ref[c, x], c, x) for x in range(nx)]
        to_z_ref[:, c * 128 : (c + 1) * 128] = lane_pick(jnp.concatenate(planes, axis=0), 127)


def pair_kernel(
    got_ref, got_rows_ref, own_ref, sums, targets, target_vec, slots, group_block, counts, features, middle_rows,
    even, odd, semaphore,
):
    blocks = own_ref.shape[0]
    peers = got_ref.shape[0] // ROWS
    total_slots = peers * SLOTS
    target_rows = got_rows_ref[pl.ds(ROWS - 1, peers, stride=ROWS), :]
    if peers < 128:
        target_rows = jnp.concatenate([target_rows, jnp.full((128 - peers, 128), -1.0)], axis=0)
    target_vec[...] = target_rows.T[0:8, :].astype(jnp.int32)
    copy = pltpu.make_async_copy(target_vec, targets, semaphore)
    copy.start()
    sums[...] = jnp.zeros(sums.shape, jnp.float32)
    sub = lax.broadcasted_iota(jnp.int32, (8, FACETS), 0)
    far = jnp.where(sub == 3, -1.0e6, 0.0)
    features[total_slots] = jnp.concatenate([far, jnp.zeros((40, FACETS), jnp.float32)], axis=0).astype(jnp.bfloat16)
    for k in range(SLOTS):
        for block in range(blocks + 1):
            counts[k][block] = 0
    for c in range(3):
        middle_rows[3 * total_slots + c] = jnp.zeros((1, FACETS), jnp.float32)
    copy.wait()

    def prepare(peer, carry):
        for k in range(SLOTS):
            target = targets[k, peer]
            block = jnp.where(target < 0, blocks, target)
            counts[k][block] = counts[k][block] + 1
            x, y, z = [
                jnp.broadcast_to(got_ref[peer * ROWS + 3 * k + c], (8, FACETS)) - CENTER for c in range(3)
            ]
            away = x * x + y * y + z * z
            value = jnp.where(sub == 4, 1.0, -away)
            for index, part in enumerate((x, y, z)):
                middle_rows[3 * (peer * SLOTS + k) + index] = part[0:1]
                value = jnp.where(sub == index, part, value)
            value = jnp.where(sub > 4, 0.0, value)
            high, middle, low = split_3(value)
            features[peer * SLOTS + k] = jnp.concatenate(
                [high, middle, low, high, middle, high], axis=0
            ).astype(jnp.bfloat16)
        return carry

    lax.fori_loop(0, peers, prepare, 0, unroll=2)
    place = 0
    for block in range(blocks):
        first = place
        for k in range(SLOTS):
            number = counts[k][block]
            counts[k][block] = place
            place = place + number
        for k in range(GROUP):
            slots[place + k] = total_slots
        place = (place + (GROUP - 1)) & ~(GROUP - 1)

        def name_groups(group, carry):
            group_block[group] = block
            return carry

        lax.fori_loop(first // GROUP, place // GROUP, name_groups, 0)
    for k in range(6 * GROUP):
        slots[place + k] = total_slots
    for k in range(6):
        group_block[place // GROUP + k] = 0
    unused = unused_from(blocks, peers)
    for k in range(SLOTS):
        number = counts[k][blocks]
        counts[k][blocks] = unused
        unused = unused + number

    def sort_peer(peer, carry):
        for k in range(SLOTS):
            target = targets[k, peer]
            block = jnp.where(target < 0, blocks, target)
            spot = counts[k][block]
            counts[k][block] = spot + 1
            slots[spot] = peer * SLOTS + k
        return carry

    lax.fori_loop(0, peers, sort_peer, 0, unroll=2)

    def reach(step, out):
        for half in range(2):
            group = 2 * step + half
            columns = [features[slots[group * GROUP + k]] for k in range(GROUP)]
            out[:, half * GROUP * FACETS : (half + 1) * GROUP * FACETS] = jnp.dot(
                own_ref[group_block[group]][:, :48],
                jnp.concatenate(columns, axis=1),
                preferred_element_type=jnp.float32,
            )

    def add(step, near):
        for half in range(2):
            group = 2 * step + half
            block = group_block[group]
            bases = [3 * slots[group * GROUP + k] for k in range(GROUP)]
            for start in range(0, FACETS, 32):
                part = slice(start, start + 32)
                total = [sums[block * 4 + q, part, :] for q in range(4)]
                for k in range(GROUP):
                    column = (half * GROUP + k) * FACETS
                    weight = jnp.maximum(near[part, column : column + FACETS], 0.0)
                    total[3] = total[3] + weight
                    for c in range(3):
                        total[c] = total[c] + weight * middle_rows[bases[k] + c]
                for q in range(4):
                    sums[block * 4 + q, part, :] = total[q]

    reach(0, even)

    def two(step, carry):
        reach(2 * step + 1, odd)
        add(2 * step, even)
        reach(2 * step + 2, even)
        add(2 * step + 1, odd)
        return carry

    lax.fori_loop(0, (place // GROUP + 3) // 4, two, 0)


def unused_from(blocks, peers):
    return SLOTS * peers + (blocks + 6) * GROUP


def pair_scratch(blocks, peers):
    return [
        pltpu.SMEM((8, 128), jnp.int32),
        pltpu.VMEM((8, 128), jnp.int32),
        pltpu.SMEM((unused_from(blocks, peers) + SLOTS * peers,), jnp.int32),
        pltpu.SMEM((SLOTS * peers // GROUP + blocks + 8,), jnp.int32),
        [pltpu.SMEM((blocks + 1,), jnp.int32) for _ in range(SLOTS)],
        pltpu.VMEM((peers * SLOTS + 1, 48, FACETS), jnp.bfloat16),
        pltpu.VMEM((3 * peers * SLOTS + 3, 1, FACETS), jnp.float32),
        pltpu.VMEM((FACETS, 2 * GROUP * FACETS), jnp.float32),
        pltpu.VMEM((FACETS, 2 * GROUP * FACETS), jnp.float32),
        pltpu.SemaphoreType.DMA,
    ]


def scatter_kernel(sums_ref, cent_ref, nodes_ref, contact_ref):
    blocks = cent_ref.shape[0] // 3
    high_iota = lax.broadcasted_iota(jnp.int32, (64, FACETS), 0)
    low_iota = lax.broadcasted_iota(jnp.int32, (256, FACETS), 0)
    contact = jnp.zeros((192, 256), jnp.float32)
    for block in range(blocks):
        left, right = ([], [])
        total = [jnp.sum(sums_ref[block * 4 + q].T, axis=0, keepdims=True) for q in range(4)]
        parts = []
        for c in range(3):
            force = (cent_ref[block * 3 + c] - CENTER) * total[3] - total[c]
            high, rest = split_2(0.25 * PENALTY * force)
            parts.append((high.astype(jnp.float32), rest.astype(jnp.float32)))
        for m in range(4):
            ids = nodes_ref[block * 4 + m : block * 4 + m + 1, :]
            here = jnp.where(low_iota == (ids & 255), 1.0, 0.0).astype(jnp.bfloat16)
            in_row = high_iota == (ids >> 8)
            for part in range(2):
                left.append(
                    jnp.concatenate(
                        [jnp.where(in_row, parts[c][part], 0.0).astype(jnp.bfloat16) for c in range(3)], axis=0
                    )
                )
                right.append(here)
        contact = contact + lax.dot_general(
            jnp.concatenate(left, axis=1), jnp.concatenate(right, axis=1), NT, preferred_element_type=jnp.float32
        )
    contact_ref[pl.ds(0, 192, stride=2), :] = contact[:, :128]
    contact_ref[pl.ds(1, 192, stride=2), :] = contact[:, 128:]


def update_kernel(
    contact_ref, upper_ref, lower_ref, from_y_ref, from_x_ref, from_z_ref, from_xz_ref, velocity_ref, disp_ref,
    mass_ref, velocity_out, disp_out,
):
    nx = velocity_ref.shape[1]
    columns = columns_of(jnp.concatenate(rows_of(from_z_ref[...]) + [from_xz_ref[...]], axis=0))
    lane = lax.broadcasted_iota(jnp.int32, (16, 128), 1)
    row = lax.broadcasted_iota(jnp.int32, (16, 128), 0)
    for c in range(3):
        for x in range(nx):
            upper = upper_ref[c, x] + jnp.where(row == 0, from_y_ref[c, x : x + 1, :], 0.0)
            lower = lower_ref[c, x] + jnp.where(row == 0, from_y_ref[3 + c, x : x + 1, :], 0.0)
            below = columns[x * 16 : x * 16 + 16, c : c + 1]
            if x == 0:
                upper = upper + from_x_ref[c]
                lower = lower + from_x_ref[3 + c]
                below = below + columns[c * 16 : c * 16 + 16, 3:4]
            internal = lower + jnp.where(lane == 0, below, pltpu.roll(upper, 1, 1))
            contact = contact_ref[c * 128 + x * 16 : c * 128 + x * 16 + 16, :]
            velocity = velocity_ref[c, x] + TIME_STEP * (contact - internal) / mass_ref[x]
            velocity_out[c, x] = velocity
            disp_out[c, x] = disp_ref[c, x] + TIME_STEP * velocity


def shifted(value, axis, step):
    count = lax.axis_size(axis)
    return lax.ppermute(value, axis, [(i, i + step) for i in range(count) if 0 <= i + step < count])


def shifted_xz(value, step):
    count_x, count_z = lax.axis_size("gx"), lax.axis_size("gz")
    pairs = [
        (i * count_z + j, (i + step) * count_z + j + step)
        for i in range(count_x)
        for j in range(count_z)
        if 0 <= i + step < count_x and 0 <= j + step < count_z
    ]
    return lax.ppermute(value, ("gx", "gz"), pairs)


def f32(*shape):
    return jax.ShapeDtypeStruct(shape, jnp.float32)


def on_device(
    velocity,
    displacement,
    mass,
    stress,
    plastic,
    yield_stress,
    facet_anchor,
    facet_nodes,
    pair_source,
    pair_dest,
    pair_target,
):
    size_x, size_y, size_z = velocity.shape[1:]
    blocks = facet_anchor.shape[3]
    pairs = pair_source.shape[3]
    peers = lax.axis_size("gx") * lax.axis_size("gz")
    flat_disp = displacement.reshape(-1, size_z)
    nodes = facet_nodes.reshape(blocks * 4, FACETS)
    anchors = facet_anchor.reshape(blocks, 3, FACETS).transpose(1, 0, 2).reshape(3 * blocks, FACETS)
    barrier = lax.optimization_barrier

    low_z, low_x, low_y = pl.pallas_call(
        faces_kernel, out_shape=(f32(1, 384), f32(48, size_z), f32(24, size_z)), compiler_params=params(8), name="faces"
    )(velocity)
    face_z = shifted(low_z, "gz", -1)
    face_x = shifted(low_x, "gx", -1)
    face_xz = shifted_xz(low_z, -1)
    centroids = pl.pallas_call(
        gather_kernel, out_shape=f32(blocks * 3, 1, FACETS), compiler_params=params(16), name="gather"
    )(flat_disp, anchors, nodes)
    send = pl.pallas_call(
        place_kernel,
        out_shape=f32(peers * ROWS, 1, FACETS),
        in_specs=[VMEM, HBM, HBM, HBM],
        out_specs=VMEM,
        scratch_shapes=[
            pltpu.SMEM((pairs,), jnp.int32),
            pltpu.SMEM((pairs,), jnp.int32),
            pltpu.SMEM((pairs,), jnp.int32),
            pltpu.SMEM((peers,), jnp.int32),
            pltpu.SMEM((peers * SLOTS,), jnp.int32),
            pltpu.SemaphoreType.DMA((3,)),
        ],
        compiler_params=params(16),
        name="place",
    )(centroids, pair_source.reshape(pairs), pair_dest.reshape(pairs), pair_target.reshape(pairs))
    send, face_x, face_z, face_xz = barrier((send, face_x, face_z, face_xz))
    got = lax.all_to_all(send, ("gx", "gz"), split_axis=0, concat_axis=0, tiled=True)
    edges = pl.pallas_call(edges_kernel, out_shape=f32(40, size_z), compiler_params=params(8), name="edges")(
        low_y, face_x, face_z, face_xz
    )
    face_y = shifted(edges, "gy", -1)
    own = pl.pallas_call(
        own_kernel,
        out_shape=jax.ShapeDtypeStruct((blocks, FACETS, 128), jnp.bfloat16),
        compiler_params=params(8),
        name="own",
    )(centroids)
    stress_new, plastic_new, upper, lower, edge_y, edge_x = pl.pallas_call(
        stress_kernel,
        out_shape=(
            f32(*stress.shape),
            f32(*plastic.shape),
            f32(*velocity.shape),
            f32(*velocity.shape),
            f32(6, size_x + 1, size_z),
            f32(6, size_y, size_z),
        ),
        compiler_params=params(16),
        name="stress",
    )(velocity, face_z, face_x, face_xz, face_y, stress, plastic, yield_stress)
    from_y = shifted(edge_y, "gy", 1)
    to_x, to_z, to_xz = pl.pallas_call(
        force_kernel,
        out_shape=(f32(6, size_y, size_z), f32(1, 384), f32(1, 128)),
        compiler_params=params(8),
        name="force",
    )(upper, edge_x, from_y)
    from_x = shifted(to_x, "gx", 1)
    from_z = shifted(to_z, "gz", 1)
    from_xz = shifted_xz(to_xz, 1)
    got, own, from_x, from_z, from_xz = barrier((got, own, from_x, from_z, from_xz))
    sums = pl.pallas_call(
        pair_kernel,
        out_shape=f32(blocks * 4, FACETS, FACETS),
        scratch_shapes=pair_scratch(blocks, peers),
        compiler_params=params(24),
        name="pairs",
    )(got, got.reshape(peers * ROWS, FACETS), own)
    contact = pl.pallas_call(
        scatter_kernel, out_shape=f32(384, 128), compiler_params=params(16), name="scatter"
    )(sums, centroids, nodes)
    velocity_new, displacement_new = pl.pallas_call(
        update_kernel,
        out_shape=(f32(*velocity.shape), f32(*velocity.shape)),
        compiler_params=params(8),
        name="update",
    )(contact, upper, lower, from_y, from_x, from_z, from_xz, velocity, displacement, mass)
    return (velocity_new, displacement_new, stress_new, plastic_new)


def solution(mesh):
    return jax.shard_map(
        on_device,
        mesh=mesh,
        in_specs=(
            P(None, "gx", "gy", "gz"),
            P(None, "gx", "gy", "gz"),
            P("gx", "gy", "gz"),
            P(None, "gx", "gy", "gz"),
            P("gx", "gy", "gz"),
            P("gx", "gy", "gz"),
            P("gx", "gy", "gz", None, None, None),
            P("gx", "gy", "gz", None, None, None),
            P("gx", "gy", "gz", None),
            P("gx", "gy", "gz", None, None),
            P("gx", "gy", "gz", None),
        ),
        out_specs=(
            P(None, "gx", "gy", "gz"),
            P(None, "gx", "gy", "gz"),
            P(None, "gx", "gy", "gz"),
            P("gx", "gy", "gz"),
        ),
        check_vma=False,
    )
```

```python
import jax
import jax.numpy as jnp
from jax import lax
from jax.experimental import pallas as pl
from jax.experimental.pallas import tpu as pltpu
from jax.sharding import PartitionSpec as P

FACETS = 128
SLOTS = 4
CENTER = 2.0
GROUP = 8
ROWS = 13
TIME_STEP = 0.25
SHEAR_MODULUS = 1.0
BULK_MODULUS = 2.0
HARDENING = 1.0
PENALTY = 1.0
REACH_SQUARED = 1.0
VOIGT = ((0, 3, 5), (3, 1, 4), (5, 4, 2))
NT = (((1,), (1,)), ((), ()))
VMEM = pl.BlockSpec(memory_space=pltpu.VMEM)
HBM = pl.BlockSpec(memory_space=pltpu.HBM)


def params(mib):
    return pltpu.CompilerParams(vmem_limit_bytes=mib * 1024 * 1024)


def split_2(value):
    high = value.astype(jnp.bfloat16)
    rest = (value - high.astype(jnp.float32)).astype(jnp.bfloat16)
    return high, rest


def lane_pick(value, lane):
    pick = (lax.broadcasted_iota(jnp.int32, (8, 128), 1) == lane).astype(jnp.float32)
    return lax.dot_general(
        pick, value, NT, precision=lax.Precision.HIGHEST, preferred_element_type=jnp.float32
    )[0:1]


def columns_of(rows):
    count = rows.shape[0]
    padded = jnp.concatenate([rows, jnp.zeros((128 - count, 128), jnp.float32)], axis=0)
    return padded.T


def rows_of(row):
    return [row[:, c * 128 : (c + 1) * 128] for c in range(row.shape[1] // 128)]


def edges_kernel(low_y_ref, face_x_ref, face_z_ref, face_xz_ref, out_ref):
    rows = [face_x_ref[c * 16 : c * 16 + 1, :] for c in range(3)]
    rows = rows + rows_of(face_z_ref[...]) + rows_of(face_xz_ref[...])
    out_ref[...] = jnp.concatenate([low_y_ref[...]] + rows + [jnp.zeros((7, 128), jnp.float32)], axis=0)


def begin_kernel(
    velocity_ref, disp_ref, anchor_ref, nodes_ref, source_hbm, dest_hbm, target_hbm,
    low_z_ref, low_x_ref, low_y_ref, cent_ref, send_ref, source_ref, dest_ref, target_ref, count, slot_target, sems,
):
    peers = send_ref.shape[0] // ROWS
    pairs = source_ref.shape[0]
    copies = [
        pltpu.make_async_copy(source_hbm, source_ref, sems.at[0]),
        pltpu.make_async_copy(dest_hbm, dest_ref, sems.at[1]),
        pltpu.make_async_copy(target_hbm, target_ref, sems.at[2]),
    ]
    for copy in copies:
        copy.start()
    for peer in range(peers):
        count[peer] = 0
    for slot in range(peers * SLOTS):
        slot_target[slot] = -1
    for c in range(3):
        planes = [velocity_ref[c, x] for x in range(velocity_ref.shape[1])]
        low_z_ref[:, c * 128 : (c + 1) * 128] = lane_pick(jnp.concatenate(planes, axis=0), 0)
        low_x_ref[c * 16 : (c + 1) * 16, :] = planes[0]
        low_y_ref[c * 8 : (c + 1) * 8, :] = jnp.concatenate([plane[0:1] for plane in planes], axis=0)
    high, rest = split_2(disp_ref[...])
    table = jnp.concatenate([high, rest], axis=1)
    iota = lax.broadcasted_iota(jnp.int32, (128, 4 * FACETS), 0)
    blocks = anchor_ref.shape[0] // 3
    for block in range(blocks):
        ids = jnp.concatenate([nodes_ref[block * 4 + m : block * 4 + m + 1, :] for m in range(4)], axis=1)
        here = jnp.where(iota == (ids & 127), 1.0, 0.0).astype(jnp.bfloat16)
        picked = jnp.dot(table, jnp.concatenate([here, here], axis=0), preferred_element_type=jnp.float32)
        in_row = iota == (ids >> 7)
        for c in range(3):
            kept = jnp.where(in_row, picked[c * 128 : (c + 1) * 128], 0.0)
            total = kept[:, :128] + kept[:, 128:256] + kept[:, 256:384] + kept[:, 384:]
            total = jnp.sum(total, axis=0, keepdims=True)
            cent_ref[block * 3 + c] = anchor_ref[c * blocks + block : c * blocks + block + 1, :] + 0.25 * total
    for copy in copies:
        copy.wait()

    def place(pair, carry):
        dest = dest_ref[pair]
        slot = count[dest]
        count[dest] = slot + 1
        slot_target[dest * SLOTS + slot] = target_ref[pair]
        send_ref[pl.ds(dest * ROWS + 3 * slot, 3)] = cent_ref[pl.ds(source_ref[pair] * 3, 3)]
        return carry

    lax.fori_loop(0, pairs, place, 0, unroll=8)
    lane = lax.broadcasted_iota(jnp.int32, (1, 128), 1)

    def write_targets(peer, carry):
        row = jnp.full((1, 128), -1, jnp.int32)
        for k in range(SLOTS):
            row = jnp.where(lane == k, slot_target[peer * SLOTS + k], row)
        send_ref[peer * ROWS + ROWS - 1] = row.astype(jnp.float32)
        return carry

    lax.fori_loop(0, peers, write_targets, 0, unroll=8)


def split_3(value):
    high = value.astype(jnp.bfloat16).astype(jnp.float32)
    rest = value - high
    middle = rest.astype(jnp.bfloat16).astype(jnp.float32)
    return high, middle, rest - middle


def own_kernel(cent_ref, own_ref):
    for block in range(own_ref.shape[0]):
        x, y, z = [cent_ref[block * 3 + c] - CENTER for c in range(3)]
        one = jnp.ones_like(x)
        rows = [2.0 * x, 2.0 * y, 2.0 * z, one, REACH_SQUARED - (x * x + y * y + z * z)]
        features = jnp.concatenate(rows + [jnp.zeros((3, FACETS), jnp.float32)], axis=0)
        high, middle, low = split_3(features)
        parts = jnp.concatenate([high, high, high, middle, middle, low, jnp.zeros((80, FACETS), jnp.float32)], axis=0)
        own_ref[block] = parts.T.astype(jnp.bfloat16)


def stress_kernel(
    velocity_ref, face_z_ref, face_x_ref, face_xz_ref, face_y_ref, stress_ref, plastic_ref, yield_ref,
    stress_out, plastic_out, upper_out, lower_out, edge_y_out, edge_x_out,
):
    nx = velocity_ref.shape[1]
    columns = columns_of(
        jnp.concatenate(rows_of(face_z_ref[...]) + rows_of(face_xz_ref[...]) + [face_y_ref[27:33, :]], axis=0)
    )
    lane = lax.broadcasted_iota(jnp.int32, (16, 128), 1)
    row = lax.broadcasted_iota(jnp.int32, (16, 128), 0)
    grad_x, grad_y, grad_z = ([], [], [])
    for c in range(3):
        sum_yz, dif_y, dif_z = ([], [], [])
        for x in range(nx + 1):
            if x < nx:
                plane = velocity_ref[c, x]
                beyond = columns[x * 16 : x * 16 + 16, c : c + 1]
                edge = face_y_ref[c * 8 + x : c * 8 + x + 1, :]
                edge_beyond = columns[x * 16 : x * 16 + 1, 6 + c : 7 + c]
            else:
                plane = face_x_ref[c * 16 : c * 16 + 16, :]
                beyond = columns[0:16, 3 + c : 4 + c]
                edge = face_y_ref[24 + c : 25 + c, :]
                edge_beyond = columns[0:1, 9 + c : 10 + c]
            edge = jnp.broadcast_to(edge, (16, 128))
            after = jnp.where(lane == 127, beyond, pltpu.roll(plane, 127, 1))
            edge_after = jnp.where(lane == 127, edge_beyond, pltpu.roll(edge, 127, 1))
            sum_z, dif = plane + after, after - plane
            sum_z_next = jnp.where(row == 15, edge + edge_after, pltpu.roll(sum_z, 15, 0))
            dif_next = jnp.where(row == 15, edge_after - edge, pltpu.roll(dif, 15, 0))
            sum_yz.append(sum_z + sum_z_next)
            dif_y.append(sum_z_next - sum_z)
            dif_z.append(dif + dif_next)
        grad_x.append([0.25 * (sum_yz[x + 1] - sum_yz[x]) for x in range(nx)])
        grad_y.append([0.25 * (dif_y[x + 1] + dif_y[x]) for x in range(nx)])
        grad_z.append([0.25 * (dif_z[x + 1] + dif_z[x]) for x in range(nx)])
    stresses = []
    for x in range(nx):
        inc = [TIME_STEP * grad_x[0][x], TIME_STEP * grad_y[1][x], TIME_STEP * grad_z[2][x]]
        shear = [
            TIME_STEP * 0.5 * (grad_y[0][x] + grad_x[1][x]),
            TIME_STEP * 0.5 * (grad_z[1][x] + grad_y[2][x]),
            TIME_STEP * 0.5 * (grad_z[0][x] + grad_x[2][x]),
        ]
        volume = inc[0] + inc[1] + inc[2]
        trial = [
            stress_ref[d, x] + 2.0 * SHEAR_MODULUS * (inc[d] - volume / 3.0) + BULK_MODULUS * volume
            for d in range(3)
        ]
        trial_shear = [stress_ref[3 + d, x] + 2.0 * SHEAR_MODULUS * shear[d] for d in range(3)]
        mean = (trial[0] + trial[1] + trial[2]) / 3.0
        dev = [trial[d] - mean for d in range(3)]
        square = dev[0] * dev[0] + dev[1] * dev[1] + dev[2] * dev[2]
        square = square + 2.0 * (
            trial_shear[0] * trial_shear[0] + trial_shear[1] * trial_shear[1] + trial_shear[2] * trial_shear[2]
        )
        equivalent = jnp.sqrt(1.5 * square)
        plastic = plastic_ref[x]
        limit = yield_ref[x] + HARDENING * plastic
        gamma = jnp.maximum(equivalent - limit, 0.0) / (3.0 * SHEAR_MODULUS + HARDENING)
        factor = 1.0 - 3.0 * SHEAR_MODULUS * gamma / jnp.maximum(equivalent, limit)
        new = [dev[d] * factor + mean for d in range(3)] + [trial_shear[d] * factor for d in range(3)]
        for d in range(6):
            stress_out[d, x] = new[d]
        plastic_out[x] = plastic + gamma
        stresses.append(new)
    for c in range(3):
        before = None
        edge_before = None
        for x in range(nx + 1):
            if x < nx:
                s = [0.25 * stresses[x][VOIGT[c][d]] for d in range(3)]
                down = [jnp.where(row == 0, 0.0, pltpu.roll(v, 1, 0)) for v in s]
                here = [down[0] + s[0], down[1] - s[1], down[2] + s[2]]
                edge_here = [v[15:16] for v in s]
            if x == 0:
                x0, x1, x2 = -here[0], here[1], here[2]
                e0, e1, e2 = -edge_here[0], edge_here[1], edge_here[2]
            elif x < nx:
                x0, x1, x2 = before[0] - here[0], before[1] + here[1], before[2] + here[2]
                e0, e1, e2 = (
                    edge_before[0] - edge_here[0], edge_before[1] + edge_here[1], edge_before[2] + edge_here[2]
                )
            else:
                x0, x1, x2 = before
                e0, e1, e2 = edge_before
            both = x0 + x1
            edge_both = e0 + e1
            if x < nx:
                upper_out[c, x] = both + x2
                lower_out[c, x] = both - x2
            else:
                edge_x_out[c] = both + x2
                edge_x_out[3 + c] = both - x2
            edge_y_out[c, x : x + 1, :] = edge_both + e2
            edge_y_out[3 + c, x : x + 1, :] = edge_both - e2
            before, edge_before = here, edge_here


def force_kernel(upper_ref, edge_x_ref, from_y_ref, to_x_ref, to_z_ref, to_xz_ref):
    nx = upper_ref.shape[1]
    row = lax.broadcasted_iota(jnp.int32, (16, 128), 0)

    def with_y(plane, c, x):
        return plane + jnp.where(row == 0, from_y_ref[c, x : x + 1, :], 0.0)

    corner = []
    for c in range(6):
        plane = with_y(edge_x_ref[c], c, nx)
        to_x_ref[c] = plane
        corner.append(plane)
    to_xz_ref[...] = lane_pick(jnp.concatenate(corner[:3] + [jnp.zeros((80, 128), jnp.float32)], axis=0), 127)
    for c in range(3):
        planes = [with_y(upper_ref[c, x], c, x) for x in range(nx)]
        to_z_ref[:, c * 128 : (c + 1) * 128] = lane_pick(jnp.concatenate(planes, axis=0), 127)


def pair_kernel(
    got_ref, got_rows_ref, own_ref, cent_ref, nodes_ref, contact_ref, sums, targets, target_vec, slots, group_block, counts, features, middle_rows,
    even, odd, semaphore,
):
    blocks = own_ref.shape[0]
    peers = got_ref.shape[0] // ROWS
    total_slots = peers * SLOTS
    target_rows = got_rows_ref[pl.ds(ROWS - 1, peers, stride=ROWS), :]
    if peers < 128:
        target_rows = jnp.concatenate([target_rows, jnp.full((128 - peers, 128), -1.0)], axis=0)
    target_vec[...] = target_rows.T[0:8, :].astype(jnp.int32)
    copy = pltpu.make_async_copy(target_vec, targets, semaphore)
    copy.start()
    sums[...] = jnp.zeros(sums.shape, jnp.float32)
    sub = lax.broadcasted_iota(jnp.int32, (8, FACETS), 0)
    far = jnp.where(sub == 3, -1.0e6, 0.0)
    features[total_slots] = jnp.concatenate([far, jnp.zeros((40, FACETS), jnp.float32)], axis=0).astype(jnp.bfloat16)
    for k in range(SLOTS):
        for block in range(blocks + 1):
            counts[k][block] = 0
    for c in range(3):
        middle_rows[3 * total_slots + c] = jnp.zeros((1, FACETS), jnp.float32)
    copy.wait()

    def prepare(peer, carry):
        for k in range(SLOTS):
            target = targets[k, peer]
            block = jnp.where(target < 0, blocks, target)
            counts[k][block] = counts[k][block] + 1
            x, y, z = [
                jnp.broadcast_to(got_ref[peer * ROWS + 3 * k + c], (8, FACETS)) - CENTER for c in range(3)
            ]
            away = x * x + y * y + z * z
            value = jnp.where(sub == 4, 1.0, -away)
            for index, part in enumerate((x, y, z)):
                middle_rows[3 * (peer * SLOTS + k) + index] = part[0:1]
                value = jnp.where(sub == index, part, value)
            value = jnp.where(sub > 4, 0.0, value)
            high, middle, low = split_3(value)
            features[peer * SLOTS + k] = jnp.concatenate(
                [high, middle, low, high, middle, high], axis=0
            ).astype(jnp.bfloat16)
        return carry

    lax.fori_loop(0, peers, prepare, 0, unroll=2)
    place = 0
    for block in range(blocks):
        first = place
        for k in range(SLOTS):
            number = counts[k][block]
            counts[k][block] = place
            place = place + number
        for k in range(GROUP):
            slots[place + k] = total_slots
        place = (place + (GROUP - 1)) & ~(GROUP - 1)

        def name_groups(group, carry):
            group_block[group] = block
            return carry

        lax.fori_loop(first // GROUP, place // GROUP, name_groups, 0)
    for k in range(6 * GROUP):
        slots[place + k] = total_slots
    for k in range(6):
        group_block[place // GROUP + k] = 0
    unused = unused_from(blocks, peers)
    for k in range(SLOTS):
        number = counts[k][blocks]
        counts[k][blocks] = unused
        unused = unused + number

    def sort_peer(peer, carry):
        for k in range(SLOTS):
            target = targets[k, peer]
            block = jnp.where(target < 0, blocks, target)
            spot = counts[k][block]
            counts[k][block] = spot + 1
            slots[spot] = peer * SLOTS + k
        return carry

    lax.fori_loop(0, peers, sort_peer, 0, unroll=2)

    def reach(step, out):
        for half in range(2):
            group = 2 * step + half
            columns = [features[slots[group * GROUP + k]] for k in range(GROUP)]
            out[:, half * GROUP * FACETS : (half + 1) * GROUP * FACETS] = jnp.dot(
                own_ref[group_block[group]][:, :48],
                jnp.concatenate(columns, axis=1),
                preferred_element_type=jnp.float32,
            )

    def add(step, near):
        for half in range(2):
            group = 2 * step + half
            block = group_block[group]
            bases = [3 * slots[group * GROUP + k] for k in range(GROUP)]
            for start in range(0, FACETS, 32):
                part = slice(start, start + 32)
                total = [sums[block * 4 + q, part, :] for q in range(4)]
                for k in range(GROUP):
                    column = (half * GROUP + k) * FACETS
                    weight = jnp.maximum(near[part, column : column + FACETS], 0.0)
                    total[3] = total[3] + weight
                    for c in range(3):
                        total[c] = total[c] + weight * middle_rows[bases[k] + c]
                for q in range(4):
                    sums[block * 4 + q, part, :] = total[q]

    reach(0, even)

    def two(step, carry):
        reach(2 * step + 1, odd)
        add(2 * step, even)
        reach(2 * step + 2, even)
        add(2 * step + 1, odd)
        return carry

    lax.fori_loop(0, (place // GROUP + 3) // 4, two, 0)
    scatter(sums, cent_ref, nodes_ref, contact_ref)


def unused_from(blocks, peers):
    return SLOTS * peers + (blocks + 6) * GROUP


def pair_scratch(blocks, peers):
    return [
        pltpu.VMEM((blocks * 4, FACETS, FACETS), jnp.float32),
        pltpu.SMEM((8, 128), jnp.int32),
        pltpu.VMEM((8, 128), jnp.int32),
        pltpu.SMEM((unused_from(blocks, peers) + SLOTS * peers,), jnp.int32),
        pltpu.SMEM((SLOTS * peers // GROUP + blocks + 8,), jnp.int32),
        [pltpu.SMEM((blocks + 1,), jnp.int32) for _ in range(SLOTS)],
        pltpu.VMEM((peers * SLOTS + 1, 48, FACETS), jnp.bfloat16),
        pltpu.VMEM((3 * peers * SLOTS + 3, 1, FACETS), jnp.float32),
        pltpu.VMEM((FACETS, 2 * GROUP * FACETS), jnp.float32),
        pltpu.VMEM((FACETS, 2 * GROUP * FACETS), jnp.float32),
        pltpu.SemaphoreType.DMA,
    ]


def scatter(sums_ref, cent_ref, nodes_ref, contact_ref):
    blocks = cent_ref.shape[0] // 3
    high_iota = lax.broadcasted_iota(jnp.int32, (64, FACETS), 0)
    low_iota = lax.broadcasted_iota(jnp.int32, (256, FACETS), 0)
    contact = jnp.zeros((192, 256), jnp.float32)
    for block in range(blocks):
        left, right = ([], [])
        total = [jnp.sum(sums_ref[block * 4 + q].T, axis=0, keepdims=True) for q in range(4)]
        parts = []
        for c in range(3):
            force = (cent_ref[block * 3 + c] - CENTER) * total[3] - total[c]
            high, rest = split_2(0.25 * PENALTY * force)
            parts.append((high.astype(jnp.float32), rest.astype(jnp.float32)))
        for m in range(4):
            ids = nodes_ref[block * 4 + m : block * 4 + m + 1, :]
            here = jnp.where(low_iota == (ids & 255), 1.0, 0.0).astype(jnp.bfloat16)
            in_row = high_iota == (ids >> 8)
            for part in range(2):
                left.append(
                    jnp.concatenate(
                        [jnp.where(in_row, parts[c][part], 0.0).astype(jnp.bfloat16) for c in range(3)], axis=0
                    )
                )
                right.append(here)
        contact = contact + lax.dot_general(
            jnp.concatenate(left, axis=1), jnp.concatenate(right, axis=1), NT, preferred_element_type=jnp.float32
        )
    contact_ref[pl.ds(0, 192, stride=2), :] = contact[:, :128]
    contact_ref[pl.ds(1, 192, stride=2), :] = contact[:, 128:]


def update_kernel(
    contact_ref, upper_ref, lower_ref, from_y_ref, from_x_ref, from_z_ref, from_xz_ref, velocity_ref, disp_ref,
    mass_ref, velocity_out, disp_out,
):
    nx = velocity_ref.shape[1]
    columns = columns_of(jnp.concatenate(rows_of(from_z_ref[...]) + [from_xz_ref[...]], axis=0))
    lane = lax.broadcasted_iota(jnp.int32, (16, 128), 1)
    row = lax.broadcasted_iota(jnp.int32, (16, 128), 0)
    for c in range(3):
        for x in range(nx):
            upper = upper_ref[c, x] + jnp.where(row == 0, from_y_ref[c, x : x + 1, :], 0.0)
            lower = lower_ref[c, x] + jnp.where(row == 0, from_y_ref[3 + c, x : x + 1, :], 0.0)
            below = columns[x * 16 : x * 16 + 16, c : c + 1]
            if x == 0:
                upper = upper + from_x_ref[c]
                lower = lower + from_x_ref[3 + c]
                below = below + columns[c * 16 : c * 16 + 16, 3:4]
            internal = lower + jnp.where(lane == 0, below, pltpu.roll(upper, 1, 1))
            contact = contact_ref[c * 128 + x * 16 : c * 128 + x * 16 + 16, :]
            velocity = velocity_ref[c, x] + TIME_STEP * (contact - internal) / mass_ref[x]
            velocity_out[c, x] = velocity
            disp_out[c, x] = disp_ref[c, x] + TIME_STEP * velocity


def shifted(value, axis, step):
    count = lax.axis_size(axis)
    return lax.ppermute(value, axis, [(i, i + step) for i in range(count) if 0 <= i + step < count])


def shifted_xz(value, step):
    count_x, count_z = lax.axis_size("gx"), lax.axis_size("gz")
    pairs = [
        (i * count_z + j, (i + step) * count_z + j + step)
        for i in range(count_x)
        for j in range(count_z)
        if 0 <= i + step < count_x and 0 <= j + step < count_z
    ]
    return lax.ppermute(value, ("gx", "gz"), pairs)


def f32(*shape):
    return jax.ShapeDtypeStruct(shape, jnp.float32)


def on_device(
    velocity,
    displacement,
    mass,
    stress,
    plastic,
    yield_stress,
    facet_anchor,
    facet_nodes,
    pair_source,
    pair_dest,
    pair_target,
):
    size_x, size_y, size_z = velocity.shape[1:]
    blocks = facet_anchor.shape[3]
    pairs = pair_source.shape[3]
    peers = lax.axis_size("gx") * lax.axis_size("gz")
    flat_disp = displacement.reshape(-1, size_z)
    nodes = facet_nodes.reshape(blocks * 4, FACETS)
    anchors = facet_anchor.reshape(blocks, 3, FACETS).transpose(1, 0, 2).reshape(3 * blocks, FACETS)
    barrier = lax.optimization_barrier

    low_z, low_x, low_y, centroids, send = pl.pallas_call(
        begin_kernel,
        out_shape=(
            f32(1, 384),
            f32(48, size_z),
            f32(24, size_z),
            f32(blocks * 3, 1, FACETS),
            f32(peers * ROWS, 1, FACETS),
        ),
        in_specs=[VMEM, VMEM, VMEM, VMEM, HBM, HBM, HBM],
        scratch_shapes=[
            pltpu.SMEM((pairs,), jnp.int32),
            pltpu.SMEM((pairs,), jnp.int32),
            pltpu.SMEM((pairs,), jnp.int32),
            pltpu.SMEM((peers,), jnp.int32),
            pltpu.SMEM((peers * SLOTS,), jnp.int32),
            pltpu.SemaphoreType.DMA((3,)),
        ],
        compiler_params=pltpu.CompilerParams(vmem_limit_bytes=64 * 1024 * 1024 - 128 * 1024),
        name="begin",
    )(
        velocity,
        flat_disp,
        anchors,
        nodes,
        pair_source.reshape(pairs),
        pair_dest.reshape(pairs),
        pair_target.reshape(pairs),
    )
    face_z = shifted(low_z, "gz", -1)
    face_x = shifted(low_x, "gx", -1)
    face_xz = shifted_xz(low_z, -1)
    send, face_x, face_z, face_xz = barrier((send, face_x, face_z, face_xz))
    got = lax.all_to_all(send, ("gx", "gz"), split_axis=0, concat_axis=0, tiled=True)
    edges = pl.pallas_call(edges_kernel, out_shape=f32(40, size_z), compiler_params=params(8), name="edges")(
        low_y, face_x, face_z, face_xz
    )
    face_y = shifted(edges, "gy", -1)
    own = pl.pallas_call(
        own_kernel,
        out_shape=jax.ShapeDtypeStruct((blocks, FACETS, 128), jnp.bfloat16),
        compiler_params=params(8),
        name="own",
    )(centroids)
    stress_new, plastic_new, upper, lower, edge_y, edge_x = pl.pallas_call(
        stress_kernel,
        out_shape=(
            f32(*stress.shape),
            f32(*plastic.shape),
            f32(*velocity.shape),
            f32(*velocity.shape),
            f32(6, size_x + 1, size_z),
            f32(6, size_y, size_z),
        ),
        compiler_params=params(16),
        name="stress",
    )(velocity, face_z, face_x, face_xz, face_y, stress, plastic, yield_stress)
    from_y = shifted(edge_y, "gy", 1)
    to_x, to_z, to_xz = pl.pallas_call(
        force_kernel,
        out_shape=(f32(6, size_y, size_z), f32(1, 384), f32(1, 128)),
        compiler_params=params(8),
        name="force",
    )(upper, edge_x, from_y)
    from_x = shifted(to_x, "gx", 1)
    from_z = shifted(to_z, "gz", 1)
    from_xz = shifted_xz(to_xz, 1)
    got, own, to_x, to_z, to_xz = barrier((got, own, to_x, to_z, to_xz))
    contact = pl.pallas_call(
        pair_kernel,
        out_shape=f32(384, 128),
        scratch_shapes=pair_scratch(blocks, peers),
        compiler_params=params(24),
        name="pairs",
    )(got, got.reshape(peers * ROWS, FACETS), own, centroids, nodes)
    velocity_new, displacement_new = pl.pallas_call(
        update_kernel,
        out_shape=(f32(*velocity.shape), f32(*velocity.shape)),
        compiler_params=params(8),
        name="update",
    )(contact, upper, lower, from_y, from_x, from_z, from_xz, velocity, displacement, mass)
    return (velocity_new, displacement_new, stress_new, plastic_new)


def solution(mesh):
    return jax.shard_map(
        on_device,
        mesh=mesh,
        in_specs=(
            P(None, "gx", "gy", "gz"),
            P(None, "gx", "gy", "gz"),
            P("gx", "gy", "gz"),
            P(None, "gx", "gy", "gz"),
            P("gx", "gy", "gz"),
            P("gx", "gy", "gz"),
            P("gx", "gy", "gz", None, None, None),
            P("gx", "gy", "gz", None, None, None),
            P("gx", "gy", "gz", None),
            P("gx", "gy", "gz", None, None),
            P("gx", "gy", "gz", None),
        ),
        out_specs=(
            P(None, "gx", "gy", "gz"),
            P(None, "gx", "gy", "gz"),
            P(None, "gx", "gy", "gz"),
            P("gx", "gy", "gz"),
        ),
        check_vma=False,
    )
```

```python
import jax
import jax.numpy as jnp
from jax import lax
from jax.experimental import pallas as pl
from jax.experimental.pallas import tpu as pltpu
from jax.sharding import PartitionSpec as P

FACETS = 128
SLOTS = 4
CENTER = 2.0
GROUP = 8
AHEAD = 4
ROWS = 13
TIME_STEP = 0.25
SHEAR_MODULUS = 1.0
BULK_MODULUS = 2.0
HARDENING = 1.0
PENALTY = 1.0
REACH_SQUARED = 1.0
VOIGT = ((0, 3, 5), (3, 1, 4), (5, 4, 2))
NT = (((1,), (1,)), ((), ()))
VMEM = pl.BlockSpec(memory_space=pltpu.VMEM)
HBM = pl.BlockSpec(memory_space=pltpu.HBM)


def params(mib):
    return pltpu.CompilerParams(vmem_limit_bytes=mib * 1024 * 1024)


def split_2(value):
    high = value.astype(jnp.bfloat16)
    rest = (value - high.astype(jnp.float32)).astype(jnp.bfloat16)
    return high, rest


def lane_pick(value, lane):
    pick = (lax.broadcasted_iota(jnp.int32, (8, 128), 1) == lane).astype(jnp.float32)
    return lax.dot_general(
        pick, value, NT, precision=lax.Precision.HIGHEST, preferred_element_type=jnp.float32
    )[0:1]


def columns_of(rows):
    count = rows.shape[0]
    padded = jnp.concatenate([rows, jnp.zeros((128 - count, 128), jnp.float32)], axis=0)
    return padded.T


def rows_of(row):
    return [row[:, c * 128 : (c + 1) * 128] for c in range(row.shape[1] // 128)]


def edges_kernel(low_y_ref, face_x_ref, face_z_ref, face_xz_ref, out_ref):
    rows = [face_x_ref[c * 16 : c * 16 + 1, :] for c in range(3)]
    rows = rows + rows_of(face_z_ref[...]) + rows_of(face_xz_ref[...])
    out_ref[...] = jnp.concatenate([low_y_ref[...]] + rows + [jnp.zeros((7, 128), jnp.float32)], axis=0)


def faces_kernel(velocity_ref, low_z_ref, low_x_ref, low_y_ref):
    for c in range(3):
        planes = [velocity_ref[c, x] for x in range(velocity_ref.shape[1])]
        low_z_ref[:, c * 128 : (c + 1) * 128] = lane_pick(jnp.concatenate(planes, axis=0), 0)
        low_x_ref[c * 16 : (c + 1) * 16, :] = planes[0]
        low_y_ref[c * 8 : (c + 1) * 8, :] = jnp.concatenate([plane[0:1] for plane in planes], axis=0)


def begin_kernel(
    disp_ref, anchor_ref, nodes_ref, source_hbm, dest_hbm, target_hbm,
    cent_ref, send_ref, source_ref, dest_ref, target_ref, count, slot_target, sems,
):
    peers = send_ref.shape[0] // ROWS
    pairs = source_ref.shape[0]
    copies = [
        pltpu.make_async_copy(source_hbm, source_ref, sems.at[0]),
        pltpu.make_async_copy(dest_hbm, dest_ref, sems.at[1]),
        pltpu.make_async_copy(target_hbm, target_ref, sems.at[2]),
    ]
    for copy in copies:
        copy.start()
    for peer in range(peers):
        count[peer] = 0
    for slot in range(peers * SLOTS):
        slot_target[slot] = -1
    high, rest = split_2(disp_ref[...])
    table = jnp.concatenate([high, rest], axis=1)
    iota = lax.broadcasted_iota(jnp.int32, (128, 4 * FACETS), 0)
    blocks = anchor_ref.shape[0] // 3
    for block in range(blocks):
        ids = jnp.concatenate([nodes_ref[block * 4 + m : block * 4 + m + 1, :] for m in range(4)], axis=1)
        here = jnp.where(iota == (ids & 127), 1.0, 0.0).astype(jnp.bfloat16)
        picked = jnp.dot(table, jnp.concatenate([here, here], axis=0), preferred_element_type=jnp.float32)
        in_row = iota == (ids >> 7)
        for c in range(3):
            kept = jnp.where(in_row, picked[c * 128 : (c + 1) * 128], 0.0)
            total = kept[:, :128] + kept[:, 128:256] + kept[:, 256:384] + kept[:, 384:]
            total = jnp.sum(total, axis=0, keepdims=True)
            cent_ref[block * 3 + c] = anchor_ref[c * blocks + block : c * blocks + block + 1, :] + 0.25 * total
    for copy in copies:
        copy.wait()

    def place(pair, carry):
        dest = dest_ref[pair]
        slot = count[dest]
        count[dest] = slot + 1
        slot_target[dest * SLOTS + slot] = target_ref[pair]
        send_ref[pl.ds(dest * ROWS + 3 * slot, 3)] = cent_ref[pl.ds(source_ref[pair] * 3, 3)]
        return carry

    lax.fori_loop(0, pairs, place, 0, unroll=8)
    lane = lax.broadcasted_iota(jnp.int32, (1, 128), 1)

    def write_targets(peer, carry):
        row = jnp.full((1, 128), -1, jnp.int32)
        for k in range(SLOTS):
            row = jnp.where(lane == k, slot_target[peer * SLOTS + k], row)
        send_ref[peer * ROWS + ROWS - 1] = row.astype(jnp.float32)
        return carry

    lax.fori_loop(0, peers, write_targets, 0, unroll=8)


def split_3(value):
    high = value.astype(jnp.bfloat16).astype(jnp.float32)
    rest = value - high
    middle = rest.astype(jnp.bfloat16).astype(jnp.float32)
    return high, middle, rest - middle


def own_kernel(cent_ref, own_ref):
    for block in range(own_ref.shape[0]):
        x, y, z = [cent_ref[block * 3 + c] - CENTER for c in range(3)]
        one = jnp.ones_like(x)
        rows = [2.0 * x, 2.0 * y, 2.0 * z, one, REACH_SQUARED - (x * x + y * y + z * z)]
        features = jnp.concatenate(rows + [jnp.zeros((3, FACETS), jnp.float32)], axis=0)
        high, middle, low = split_3(features)
        parts = jnp.concatenate([high, high, high, middle, middle, low, jnp.zeros((80, FACETS), jnp.float32)], axis=0)
        own_ref[block] = parts.T.astype(jnp.bfloat16)


def stress_kernel(
    velocity_ref, face_z_ref, face_x_ref, face_xz_ref, face_y_ref, stress_ref, plastic_ref, yield_ref,
    stress_out, plastic_out, upper_out, lower_out, edge_y_out, edge_x_out,
):
    nx = velocity_ref.shape[1]
    columns = columns_of(
        jnp.concatenate(rows_of(face_z_ref[...]) + rows_of(face_xz_ref[...]) + [face_y_ref[27:33, :]], axis=0)
    )
    lane = lax.broadcasted_iota(jnp.int32, (16, 128), 1)
    row = lax.broadcasted_iota(jnp.int32, (16, 128), 0)
    grad_x, grad_y, grad_z = ([], [], [])
    for c in range(3):
        sum_yz, dif_y, dif_z = ([], [], [])
        for x in range(nx + 1):
            if x < nx:
                plane = velocity_ref[c, x]
                beyond = columns[x * 16 : x * 16 + 16, c : c + 1]
                edge = face_y_ref[c * 8 + x : c * 8 + x + 1, :]
                edge_beyond = columns[x * 16 : x * 16 + 1, 6 + c : 7 + c]
            else:
                plane = face_x_ref[c * 16 : c * 16 + 16, :]
                beyond = columns[0:16, 3 + c : 4 + c]
                edge = face_y_ref[24 + c : 25 + c, :]
                edge_beyond = columns[0:1, 9 + c : 10 + c]
            edge = jnp.broadcast_to(edge, (16, 128))
            after = jnp.where(lane == 127, beyond, pltpu.roll(plane, 127, 1))
            edge_after = jnp.where(lane == 127, edge_beyond, pltpu.roll(edge, 127, 1))
            sum_z, dif = plane + after, after - plane
            sum_z_next = jnp.where(row == 15, edge + edge_after, pltpu.roll(sum_z, 15, 0))
            dif_next = jnp.where(row == 15, edge_after - edge, pltpu.roll(dif, 15, 0))
            sum_yz.append(sum_z + sum_z_next)
            dif_y.append(sum_z_next - sum_z)
            dif_z.append(dif + dif_next)
        grad_x.append([0.25 * (sum_yz[x + 1] - sum_yz[x]) for x in range(nx)])
        grad_y.append([0.25 * (dif_y[x + 1] + dif_y[x]) for x in range(nx)])
        grad_z.append([0.25 * (dif_z[x + 1] + dif_z[x]) for x in range(nx)])
    stresses = []
    for x in range(nx):
        inc = [TIME_STEP * grad_x[0][x], TIME_STEP * grad_y[1][x], TIME_STEP * grad_z[2][x]]
        shear = [
            TIME_STEP * 0.5 * (grad_y[0][x] + grad_x[1][x]),
            TIME_STEP * 0.5 * (grad_z[1][x] + grad_y[2][x]),
            TIME_STEP * 0.5 * (grad_z[0][x] + grad_x[2][x]),
        ]
        volume = inc[0] + inc[1] + inc[2]
        trial = [
            stress_ref[d, x] + 2.0 * SHEAR_MODULUS * (inc[d] - volume / 3.0) + BULK_MODULUS * volume
            for d in range(3)
        ]
        trial_shear = [stress_ref[3 + d, x] + 2.0 * SHEAR_MODULUS * shear[d] for d in range(3)]
        mean = (trial[0] + trial[1] + trial[2]) / 3.0
        dev = [trial[d] - mean for d in range(3)]
        square = dev[0] * dev[0] + dev[1] * dev[1] + dev[2] * dev[2]
        square = square + 2.0 * (
            trial_shear[0] * trial_shear[0] + trial_shear[1] * trial_shear[1] + trial_shear[2] * trial_shear[2]
        )
        equivalent = jnp.sqrt(1.5 * square)
        plastic = plastic_ref[x]
        limit = yield_ref[x] + HARDENING * plastic
        gamma = jnp.maximum(equivalent - limit, 0.0) / (3.0 * SHEAR_MODULUS + HARDENING)
        factor = 1.0 - 3.0 * SHEAR_MODULUS * gamma / jnp.maximum(equivalent, limit)
        new = [dev[d] * factor + mean for d in range(3)] + [trial_shear[d] * factor for d in range(3)]
        for d in range(6):
            stress_out[d, x] = new[d]
        plastic_out[x] = plastic + gamma
        stresses.append(new)
    for c in range(3):
        before = None
        edge_before = None
        for x in range(nx + 1):
            if x < nx:
                s = [0.25 * stresses[x][VOIGT[c][d]] for d in range(3)]
                down = [jnp.where(row == 0, 0.0, pltpu.roll(v, 1, 0)) for v in s]
                here = [down[0] + s[0], down[1] - s[1], down[2] + s[2]]
                edge_here = [v[15:16] for v in s]
            if x == 0:
                x0, x1, x2 = -here[0], here[1], here[2]
                e0, e1, e2 = -edge_here[0], edge_here[1], edge_here[2]
            elif x < nx:
                x0, x1, x2 = before[0] - here[0], before[1] + here[1], before[2] + here[2]
                e0, e1, e2 = (
                    edge_before[0] - edge_here[0], edge_before[1] + edge_here[1], edge_before[2] + edge_here[2]
                )
            else:
                x0, x1, x2 = before
                e0, e1, e2 = edge_before
            both = x0 + x1
            edge_both = e0 + e1
            if x < nx:
                upper_out[c, x] = both + x2
                lower_out[c, x] = both - x2
            else:
                edge_x_out[c] = both + x2
                edge_x_out[3 + c] = both - x2
            edge_y_out[c, x : x + 1, :] = edge_both + e2
            edge_y_out[3 + c, x : x + 1, :] = edge_both - e2
            before, edge_before = here, edge_here


def force_kernel(upper_ref, edge_x_ref, from_y_ref, to_x_ref, to_z_ref, to_xz_ref):
    nx = upper_ref.shape[1]
    row = lax.broadcasted_iota(jnp.int32, (16, 128), 0)

    def with_y(plane, c, x):
        return plane + jnp.where(row == 0, from_y_ref[c, x : x + 1, :], 0.0)

    corner = []
    for c in range(6):
        plane = with_y(edge_x_ref[c], c, nx)
        to_x_ref[c] = plane
        corner.append(plane)
    to_xz_ref[...] = lane_pick(jnp.concatenate(corner[:3] + [jnp.zeros((80, 128), jnp.float32)], axis=0), 127)
    for c in range(3):
        planes = [with_y(upper_ref[c, x], c, x) for x in range(nx)]
        to_z_ref[:, c * 128 : (c + 1) * 128] = lane_pick(jnp.concatenate(planes, axis=0), 127)


def pair_kernel(
    got_ref, got_rows_ref, own_ref, cent_ref, nodes_ref, contact_ref, sums, targets, target_vec, slots, group_block, counts, features, middle_rows,
    near, semaphore,
):
    blocks = own_ref.shape[0]
    peers = got_ref.shape[0] // ROWS
    total_slots = peers * SLOTS
    target_rows = got_rows_ref[pl.ds(ROWS - 1, peers, stride=ROWS), :]
    if peers < 128:
        target_rows = jnp.concatenate([target_rows, jnp.full((128 - peers, 128), -1.0)], axis=0)
    target_rows = target_rows.T[0:8, :].astype(jnp.int32)
    lane = lax.broadcasted_iota(jnp.int32, (8, 128), 1)
    tally = jnp.zeros((8, 128), jnp.float32)
    for block in range(blocks):
        number = jnp.sum(jnp.where(target_rows == block, 1.0, 0.0), axis=1, keepdims=True)
        tally = jnp.where(lane == block, number, tally)
    target_vec[0:8, :] = target_rows
    target_vec[8:16, :] = tally.astype(jnp.int32)
    copy = pltpu.make_async_copy(target_vec, targets, semaphore)
    copy.start()
    sums[...] = jnp.zeros(sums.shape, jnp.float32)
    sub = lax.broadcasted_iota(jnp.int32, (8, FACETS), 0)
    far = jnp.where(sub == 3, -1.0e6, 0.0)
    features[total_slots] = jnp.concatenate([far, jnp.zeros((40, FACETS), jnp.float32)], axis=0).astype(jnp.bfloat16)
    for c in range(3):
        middle_rows[3 * total_slots + c] = jnp.zeros((1, FACETS), jnp.float32)
    copy.wait()
    place = 0
    for block in range(blocks):
        first = place
        for k in range(SLOTS):
            counts[k][block] = place
            place = place + targets[8 + k, block]
        for k in range(GROUP):
            slots[place + k] = total_slots
        place = (place + (GROUP - 1)) & ~(GROUP - 1)

        def name_groups(group, carry):
            group_block[group] = block
            return carry

        lax.fori_loop(first // GROUP, place // GROUP, name_groups, 0)
    for k in range(2 * AHEAD * GROUP):
        slots[place + k] = total_slots
    for k in range(2 * AHEAD):
        group_block[place // GROUP + k] = 0
    for k in range(SLOTS):
        counts[k][blocks] = unused_from(blocks, peers) + k * peers

    def prepare(peer, carry):
        for k in range(SLOTS):
            target = targets[k, peer]
            block = jnp.where(target < 0, blocks, target)
            spot = counts[k][block]
            counts[k][block] = spot + 1
            slots[spot] = peer * SLOTS + k
            x, y, z = [
                jnp.broadcast_to(got_ref[peer * ROWS + 3 * k + c], (8, FACETS)) - CENTER for c in range(3)
            ]
            away = x * x + y * y + z * z
            value = jnp.where(sub == 4, 1.0, -away)
            for index, part in enumerate((x, y, z)):
                middle_rows[3 * (peer * SLOTS + k) + index] = part[0:1]
                value = jnp.where(sub == index, part, value)
            value = jnp.where(sub > 4, 0.0, value)
            high, middle, low = split_3(value)
            features[peer * SLOTS + k] = jnp.concatenate(
                [high, middle, low, high, middle, high], axis=0
            ).astype(jnp.bfloat16)
        return carry

    lax.fori_loop(0, peers, prepare, 0, unroll=2)

    def reach(group, out):
        columns = [features[slots[group * GROUP + k]] for k in range(GROUP)]
        out[...] = jnp.dot(
            own_ref[group_block[group]][:, :48], jnp.concatenate(columns, axis=1), preferred_element_type=jnp.float32
        )

    def add(group, near):
        block = group_block[group]
        bases = [3 * slots[group * GROUP + k] for k in range(GROUP)]
        for start in range(0, FACETS, 32):
            part = slice(start, start + 32)
            total = [sums[block * 4 + q, part, :] for q in range(4)]
            for k in range(GROUP):
                weight = jnp.maximum(near[part, k * FACETS : (k + 1) * FACETS], 0.0)
                total[3] = total[3] + weight
                for c in range(3):
                    total[c] = total[c] + weight * middle_rows[bases[k] + c]
            for q in range(4):
                sums[block * 4 + q, part, :] = total[q]

    for i in range(AHEAD):
        reach(i, near[i])

    def some(step, carry):
        for i in range(AHEAD):
            add(step * AHEAD + i, near[i])
            reach((step + 1) * AHEAD + i, near[i])
        return carry

    lax.fori_loop(0, (place // GROUP + (AHEAD - 1)) // AHEAD, some, 0)
    scatter(sums, cent_ref, nodes_ref, contact_ref)


def unused_from(blocks, peers):
    return SLOTS * peers + (blocks + 2 * AHEAD) * GROUP


def pair_scratch(blocks, peers):
    return [
        pltpu.VMEM((blocks * 4, FACETS, FACETS), jnp.float32),
        pltpu.SMEM((16, 128), jnp.int32),
        pltpu.VMEM((16, 128), jnp.int32),
        pltpu.SMEM((unused_from(blocks, peers) + SLOTS * peers,), jnp.int32),
        pltpu.SMEM((SLOTS * peers // GROUP + blocks + 2 * AHEAD,), jnp.int32),
        [pltpu.SMEM((blocks + 1,), jnp.int32) for _ in range(SLOTS)],
        pltpu.VMEM((peers * SLOTS + 1, 48, FACETS), jnp.bfloat16),
        pltpu.VMEM((3 * peers * SLOTS + 3, 1, FACETS), jnp.float32),
        [pltpu.VMEM((FACETS, GROUP * FACETS), jnp.float32) for _ in range(AHEAD)],
        pltpu.SemaphoreType.DMA,
    ]


def scatter(sums_ref, cent_ref, nodes_ref, contact_ref):
    blocks = cent_ref.shape[0] // 3
    high_iota = lax.broadcasted_iota(jnp.int32, (64, FACETS), 0)
    low_iota = lax.broadcasted_iota(jnp.int32, (256, FACETS), 0)
    contact = jnp.zeros((192, 256), jnp.float32)
    for block in range(blocks):
        left, right = ([], [])
        total = [jnp.sum(sums_ref[block * 4 + q].T, axis=0, keepdims=True) for q in range(4)]
        parts = []
        for c in range(3):
            force = (cent_ref[block * 3 + c] - CENTER) * total[3] - total[c]
            high, rest = split_2(0.25 * PENALTY * force)
            parts.append((high.astype(jnp.float32), rest.astype(jnp.float32)))
        for m in range(4):
            ids = nodes_ref[block * 4 + m : block * 4 + m + 1, :]
            here = jnp.where(low_iota == (ids & 255), 1.0, 0.0).astype(jnp.bfloat16)
            in_row = high_iota == (ids >> 8)
            for part in range(2):
                left.append(
                    jnp.concatenate(
                        [jnp.where(in_row, parts[c][part], 0.0).astype(jnp.bfloat16) for c in range(3)], axis=0
                    )
                )
                right.append(here)
        contact = contact + lax.dot_general(
            jnp.concatenate(left, axis=1), jnp.concatenate(right, axis=1), NT, preferred_element_type=jnp.float32
        )
    contact_ref[pl.ds(0, 192, stride=2), :] = contact[:, :128]
    contact_ref[pl.ds(1, 192, stride=2), :] = contact[:, 128:]


def update_kernel(
    contact_ref, upper_ref, lower_ref, from_y_ref, from_x_ref, from_z_ref, from_xz_ref, velocity_ref, disp_ref,
    mass_ref, velocity_out, disp_out,
):
    nx = velocity_ref.shape[1]
    columns = columns_of(jnp.concatenate(rows_of(from_z_ref[...]) + [from_xz_ref[...]], axis=0))
    lane = lax.broadcasted_iota(jnp.int32, (16, 128), 1)
    row = lax.broadcasted_iota(jnp.int32, (16, 128), 0)
    for c in range(3):
        for x in range(nx):
            upper = upper_ref[c, x] + jnp.where(row == 0, from_y_ref[c, x : x + 1, :], 0.0)
            lower = lower_ref[c, x] + jnp.where(row == 0, from_y_ref[3 + c, x : x + 1, :], 0.0)
            below = columns[x * 16 : x * 16 + 16, c : c + 1]
            if x == 0:
                upper = upper + from_x_ref[c]
                lower = lower + from_x_ref[3 + c]
                below = below + columns[c * 16 : c * 16 + 16, 3:4]
            internal = lower + jnp.where(lane == 0, below, pltpu.roll(upper, 1, 1))
            contact = contact_ref[c * 128 + x * 16 : c * 128 + x * 16 + 16, :]
            velocity = velocity_ref[c, x] + TIME_STEP * (contact - internal) / mass_ref[x]
            velocity_out[c, x] = velocity
            disp_out[c, x] = disp_ref[c, x] + TIME_STEP * velocity


def shifted(value, axis, step):
    count = lax.axis_size(axis)
    return lax.ppermute(value, axis, [(i, i + step) for i in range(count) if 0 <= i + step < count])


def shifted_xz(value, step):
    count_x, count_z = lax.axis_size("gx"), lax.axis_size("gz")
    pairs = [
        (i * count_z + j, (i + step) * count_z + j + step)
        for i in range(count_x)
        for j in range(count_z)
        if 0 <= i + step < count_x and 0 <= j + step < count_z
    ]
    return lax.ppermute(value, ("gx", "gz"), pairs)


def f32(*shape):
    return jax.ShapeDtypeStruct(shape, jnp.float32)


def on_device(
    velocity,
    displacement,
    mass,
    stress,
    plastic,
    yield_stress,
    facet_anchor,
    facet_nodes,
    pair_source,
    pair_dest,
    pair_target,
):
    size_x, size_y, size_z = velocity.shape[1:]
    blocks = facet_anchor.shape[3]
    pairs = pair_source.shape[3]
    peers = lax.axis_size("gx") * lax.axis_size("gz")
    flat_disp = displacement.reshape(-1, size_z)
    nodes = facet_nodes.reshape(blocks * 4, FACETS)
    anchors = facet_anchor.reshape(blocks, 3, FACETS).transpose(1, 0, 2).reshape(3 * blocks, FACETS)
    barrier = lax.optimization_barrier

    low_z, low_x, low_y = pl.pallas_call(
        faces_kernel, out_shape=(f32(1, 384), f32(48, size_z), f32(24, size_z)), compiler_params=params(8), name="faces"
    )(velocity)
    centroids, send = pl.pallas_call(
        begin_kernel,
        out_shape=(
            f32(blocks * 3, 1, FACETS),
            f32(peers * ROWS, 1, FACETS),
        ),
        in_specs=[VMEM, VMEM, VMEM, HBM, HBM, HBM],
        scratch_shapes=[
            pltpu.SMEM((pairs,), jnp.int32),
            pltpu.SMEM((pairs,), jnp.int32),
            pltpu.SMEM((pairs,), jnp.int32),
            pltpu.SMEM((peers,), jnp.int32),
            pltpu.SMEM((peers * SLOTS,), jnp.int32),
            pltpu.SemaphoreType.DMA((3,)),
        ],
        compiler_params=pltpu.CompilerParams(vmem_limit_bytes=64 * 1024 * 1024 - 128 * 1024),
        name="begin",
    )(
        flat_disp,
        anchors,
        nodes,
        pair_source.reshape(pairs),
        pair_dest.reshape(pairs),
        pair_target.reshape(pairs),
    )
    face_z = shifted(low_z, "gz", -1)
    face_x = shifted(low_x, "gx", -1)
    face_xz = shifted_xz(low_z, -1)
    send, face_x, face_z, face_xz = barrier((send, face_x, face_z, face_xz))
    got = lax.all_to_all(send, ("gx", "gz"), split_axis=0, concat_axis=0, tiled=True)
    edges = pl.pallas_call(edges_kernel, out_shape=f32(40, size_z), compiler_params=params(8), name="edges")(
        low_y, face_x, face_z, face_xz
    )
    face_y = shifted(edges, "gy", -1)
    own = pl.pallas_call(
        own_kernel,
        out_shape=jax.ShapeDtypeStruct((blocks, FACETS, 128), jnp.bfloat16),
        compiler_params=params(8),
        name="own",
    )(centroids)
    stress_new, plastic_new, upper, lower, edge_y, edge_x = pl.pallas_call(
        stress_kernel,
        out_shape=(
            f32(*stress.shape),
            f32(*plastic.shape),
            f32(*velocity.shape),
            f32(*velocity.shape),
            f32(6, size_x + 1, size_z),
            f32(6, size_y, size_z),
        ),
        compiler_params=params(16),
        name="stress",
    )(velocity, face_z, face_x, face_xz, face_y, stress, plastic, yield_stress)
    from_y = shifted(edge_y, "gy", 1)
    to_x, to_z, to_xz = pl.pallas_call(
        force_kernel,
        out_shape=(f32(6, size_y, size_z), f32(1, 384), f32(1, 128)),
        compiler_params=params(8),
        name="force",
    )(upper, edge_x, from_y)
    from_x = shifted(to_x, "gx", 1)
    from_z = shifted(to_z, "gz", 1)
    from_xz = shifted_xz(to_xz, 1)
    got, own, to_x, to_z, to_xz = barrier((got, own, to_x, to_z, to_xz))
    contact = pl.pallas_call(
        pair_kernel,
        out_shape=f32(384, 128),
        scratch_shapes=pair_scratch(blocks, peers),
        compiler_params=params(24),
        name="pairs",
    )(got, got.reshape(peers * ROWS, FACETS), own, centroids, nodes)
    velocity_new, displacement_new = pl.pallas_call(
        update_kernel,
        out_shape=(f32(*velocity.shape), f32(*velocity.shape)),
        compiler_params=params(8),
        name="update",
    )(contact, upper, lower, from_y, from_x, from_z, from_xz, velocity, displacement, mass)
    return (velocity_new, displacement_new, stress_new, plastic_new)


def solution(mesh):
    return jax.shard_map(
        on_device,
        mesh=mesh,
        in_specs=(
            P(None, "gx", "gy", "gz"),
            P(None, "gx", "gy", "gz"),
            P("gx", "gy", "gz"),
            P(None, "gx", "gy", "gz"),
            P("gx", "gy", "gz"),
            P("gx", "gy", "gz"),
            P("gx", "gy", "gz", None, None, None),
            P("gx", "gy", "gz", None, None, None),
            P("gx", "gy", "gz", None),
            P("gx", "gy", "gz", None, None),
            P("gx", "gy", "gz", None),
        ),
        out_specs=(
            P(None, "gx", "gy", "gz"),
            P(None, "gx", "gy", "gz"),
            P(None, "gx", "gy", "gz"),
            P("gx", "gy", "gz"),
        ),
        check_vma=False,
    )
```

```python
import jax
import jax.numpy as jnp
from jax import lax
from jax.experimental import pallas as pl
from jax.experimental.pallas import tpu as pltpu
from jax.sharding import PartitionSpec as P

FACETS = 128
SLOTS = 4
CENTER = 2.0
GROUP = 8
AHEAD = 4
ROWS = 13
TIME_STEP = 0.25
SHEAR_MODULUS = 1.0
BULK_MODULUS = 2.0
HARDENING = 1.0
PENALTY = 1.0
REACH_SQUARED = 1.0
VOIGT = ((0, 3, 5), (3, 1, 4), (5, 4, 2))
NT = (((1,), (1,)), ((), ()))
VMEM = pl.BlockSpec(memory_space=pltpu.VMEM)
HBM = pl.BlockSpec(memory_space=pltpu.HBM)


def params(mib):
    return pltpu.CompilerParams(vmem_limit_bytes=mib * 1024 * 1024)


def split_2(value):
    high = value.astype(jnp.bfloat16)
    rest = (value - high.astype(jnp.float32)).astype(jnp.bfloat16)
    return high, rest


def lane_pick(value, lane):
    pick = (lax.broadcasted_iota(jnp.int32, (8, 128), 1) == lane).astype(jnp.float32)
    return lax.dot_general(
        pick, value, NT, precision=lax.Precision.HIGHEST, preferred_element_type=jnp.float32
    )[0:1]


def columns_of(rows):
    count = rows.shape[0]
    padded = jnp.concatenate([rows, jnp.zeros((128 - count, 128), jnp.float32)], axis=0)
    return padded.T


def rows_of(row):
    return [row[:, c * 128 : (c + 1) * 128] for c in range(row.shape[1] // 128)]


def edges_kernel(low_y_ref, face_x_ref, face_z_ref, face_xz_ref, out_ref):
    rows = [face_x_ref[c * 16 : c * 16 + 1, :] for c in range(3)]
    rows = rows + rows_of(face_z_ref[...]) + rows_of(face_xz_ref[...])
    out_ref[...] = jnp.concatenate([low_y_ref[...]] + rows + [jnp.zeros((7, 128), jnp.float32)], axis=0)


def faces_kernel(velocity_ref, low_z_ref, low_x_ref, low_y_ref):
    for c in range(3):
        planes = [velocity_ref[c, x] for x in range(velocity_ref.shape[1])]
        low_z_ref[:, c * 128 : (c + 1) * 128] = lane_pick(jnp.concatenate(planes, axis=0), 0)
        low_x_ref[c * 16 : (c + 1) * 16, :] = planes[0]
        low_y_ref[c * 8 : (c + 1) * 8, :] = jnp.concatenate([plane[0:1] for plane in planes], axis=0)


def begin_kernel(
    disp_ref, anchor_ref, nodes_ref, source_hbm, dest_hbm, target_hbm,
    cent_ref, send_ref, source_ref, dest_ref, target_ref, count, slot_target, sems,
):
    peers = send_ref.shape[0] // ROWS
    pairs = source_ref.shape[0]
    copies = [
        pltpu.make_async_copy(source_hbm, source_ref, sems.at[0]),
        pltpu.make_async_copy(dest_hbm, dest_ref, sems.at[1]),
        pltpu.make_async_copy(target_hbm, target_ref, sems.at[2]),
    ]
    for copy in copies:
        copy.start()
    for peer in range(peers):
        count[peer] = 0
    for slot in range(peers * SLOTS):
        slot_target[slot] = -1
    high, rest = split_2(disp_ref[...])
    table = jnp.concatenate([high, rest], axis=1)
    iota = lax.broadcasted_iota(jnp.int32, (128, 4 * FACETS), 0)
    blocks = anchor_ref.shape[0] // 3
    for block in range(blocks):
        ids = jnp.concatenate([nodes_ref[block * 4 + m : block * 4 + m + 1, :] for m in range(4)], axis=1)
        here = jnp.where(iota == (ids & 127), 1.0, 0.0).astype(jnp.bfloat16)
        picked = jnp.dot(table, jnp.concatenate([here, here], axis=0), preferred_element_type=jnp.float32)
        in_row = iota == (ids >> 7)
        for c in range(3):
            kept = jnp.where(in_row, picked[c * 128 : (c + 1) * 128], 0.0)
            total = kept[:, :128] + kept[:, 128:256] + kept[:, 256:384] + kept[:, 384:]
            total = jnp.sum(total, axis=0, keepdims=True)
            cent_ref[block * 3 + c] = anchor_ref[c * blocks + block : c * blocks + block + 1, :] + 0.25 * total
    for copy in copies:
        copy.wait()

    def place(pair, carry):
        dest = dest_ref[pair]
        slot = count[dest]
        count[dest] = slot + 1
        slot_target[dest * SLOTS + slot] = target_ref[pair]
        send_ref[pl.ds(dest * ROWS + 3 * slot, 3)] = cent_ref[pl.ds(source_ref[pair] * 3, 3)]
        return carry

    lax.fori_loop(0, pairs, place, 0, unroll=8)
    lane = lax.broadcasted_iota(jnp.int32, (1, 128), 1)

    def write_targets(peer, carry):
        row = jnp.full((1, 128), -1, jnp.int32)
        for k in range(SLOTS):
            row = jnp.where(lane == k, slot_target[peer * SLOTS + k], row)
        send_ref[peer * ROWS + ROWS - 1] = row.astype(jnp.float32)
        return carry

    lax.fori_loop(0, peers, write_targets, 0, unroll=8)


def split_3(value):
    high = value.astype(jnp.bfloat16).astype(jnp.float32)
    rest = value - high
    middle = rest.astype(jnp.bfloat16).astype(jnp.float32)
    return high, middle, rest - middle


def own_kernel(cent_ref, own_ref):
    for block in range(own_ref.shape[0]):
        x, y, z = [cent_ref[block * 3 + c] - CENTER for c in range(3)]
        one = jnp.ones_like(x)
        rows = [2.0 * x, 2.0 * y, 2.0 * z, one, REACH_SQUARED - (x * x + y * y + z * z)]
        features = jnp.concatenate(rows + [jnp.zeros((3, FACETS), jnp.float32)], axis=0)
        high, middle, low = split_3(features)
        parts = jnp.concatenate([high, high, high, middle, middle, low, jnp.zeros((80, FACETS), jnp.float32)], axis=0)
        own_ref[block] = parts.T.astype(jnp.bfloat16)


def stress_kernel(
    velocity_ref, face_z_ref, face_x_ref, face_xz_ref, face_y_ref, stress_ref, plastic_ref, yield_ref,
    stress_out, plastic_out, upper_out, lower_out, edge_y_out, edge_x_out,
):
    nx = velocity_ref.shape[1]
    columns = columns_of(
        jnp.concatenate(rows_of(face_z_ref[...]) + rows_of(face_xz_ref[...]) + [face_y_ref[27:33, :]], axis=0)
    )
    lane = lax.broadcasted_iota(jnp.int32, (16, 128), 1)
    row = lax.broadcasted_iota(jnp.int32, (16, 128), 0)
    grad_x, grad_y, grad_z = ([], [], [])
    for c in range(3):
        sum_yz, dif_y, dif_z = ([], [], [])
        for x in range(nx + 1):
            if x < nx:
                plane = velocity_ref[c, x]
                beyond = columns[x * 16 : x * 16 + 16, c : c + 1]
                edge = face_y_ref[c * 8 + x : c * 8 + x + 1, :]
                edge_beyond = columns[x * 16 : x * 16 + 1, 6 + c : 7 + c]
            else:
                plane = face_x_ref[c * 16 : c * 16 + 16, :]
                beyond = columns[0:16, 3 + c : 4 + c]
                edge = face_y_ref[24 + c : 25 + c, :]
                edge_beyond = columns[0:1, 9 + c : 10 + c]
            edge = jnp.broadcast_to(edge, (16, 128))
            after = jnp.where(lane == 127, beyond, pltpu.roll(plane, 127, 1))
            edge_after = jnp.where(lane == 127, edge_beyond, pltpu.roll(edge, 127, 1))
            sum_z, dif = plane + after, after - plane
            sum_z_next = jnp.where(row == 15, edge + edge_after, pltpu.roll(sum_z, 15, 0))
            dif_next = jnp.where(row == 15, edge_after - edge, pltpu.roll(dif, 15, 0))
            sum_yz.append(sum_z + sum_z_next)
            dif_y.append(sum_z_next - sum_z)
            dif_z.append(dif + dif_next)
        grad_x.append([0.25 * (sum_yz[x + 1] - sum_yz[x]) for x in range(nx)])
        grad_y.append([0.25 * (dif_y[x + 1] + dif_y[x]) for x in range(nx)])
        grad_z.append([0.25 * (dif_z[x + 1] + dif_z[x]) for x in range(nx)])
    stresses = []
    for x in range(nx):
        inc = [TIME_STEP * grad_x[0][x], TIME_STEP * grad_y[1][x], TIME_STEP * grad_z[2][x]]
        shear = [
            TIME_STEP * 0.5 * (grad_y[0][x] + grad_x[1][x]),
            TIME_STEP * 0.5 * (grad_z[1][x] + grad_y[2][x]),
            TIME_STEP * 0.5 * (grad_z[0][x] + grad_x[2][x]),
        ]
        volume = inc[0] + inc[1] + inc[2]
        trial = [
            stress_ref[d, x] + 2.0 * SHEAR_MODULUS * (inc[d] - volume / 3.0) + BULK_MODULUS * volume
            for d in range(3)
        ]
        trial_shear = [stress_ref[3 + d, x] + 2.0 * SHEAR_MODULUS * shear[d] for d in range(3)]
        mean = (trial[0] + trial[1] + trial[2]) / 3.0
        dev = [trial[d] - mean for d in range(3)]
        square = dev[0] * dev[0] + dev[1] * dev[1] + dev[2] * dev[2]
        square = square + 2.0 * (
            trial_shear[0] * trial_shear[0] + trial_shear[1] * trial_shear[1] + trial_shear[2] * trial_shear[2]
        )
        equivalent = jnp.sqrt(1.5 * square)
        plastic = plastic_ref[x]
        limit = yield_ref[x] + HARDENING * plastic
        gamma = jnp.maximum(equivalent - limit, 0.0) / (3.0 * SHEAR_MODULUS + HARDENING)
        factor = 1.0 - 3.0 * SHEAR_MODULUS * gamma / jnp.maximum(equivalent, limit)
        new = [dev[d] * factor + mean for d in range(3)] + [trial_shear[d] * factor for d in range(3)]
        for d in range(6):
            stress_out[d, x] = new[d]
        plastic_out[x] = plastic + gamma
        stresses.append(new)
    for c in range(3):
        before = None
        edge_before = None
        for x in range(nx + 1):
            if x < nx:
                s = [0.25 * stresses[x][VOIGT[c][d]] for d in range(3)]
                down = [jnp.where(row == 0, 0.0, pltpu.roll(v, 1, 0)) for v in s]
                here = [down[0] + s[0], down[1] - s[1], down[2] + s[2]]
                edge_here = [v[15:16] for v in s]
            if x == 0:
                x0, x1, x2 = -here[0], here[1], here[2]
                e0, e1, e2 = -edge_here[0], edge_here[1], edge_here[2]
            elif x < nx:
                x0, x1, x2 = before[0] - here[0], before[1] + here[1], before[2] + here[2]
                e0, e1, e2 = (
                    edge_before[0] - edge_here[0], edge_before[1] + edge_here[1], edge_before[2] + edge_here[2]
                )
            else:
                x0, x1, x2 = before
                e0, e1, e2 = edge_before
            both = x0 + x1
            edge_both = e0 + e1
            if x < nx:
                upper_out[c, x] = both + x2
                lower_out[c, x] = both - x2
            else:
                edge_x_out[c] = both + x2
                edge_x_out[3 + c] = both - x2
            edge_y_out[c, x : x + 1, :] = edge_both + e2
            edge_y_out[3 + c, x : x + 1, :] = edge_both - e2
            before, edge_before = here, edge_here


def force_kernel(upper_ref, edge_x_ref, from_y_ref, to_x_ref, to_z_ref, to_xz_ref):
    nx = upper_ref.shape[1]
    row = lax.broadcasted_iota(jnp.int32, (16, 128), 0)

    def with_y(plane, c, x):
        return plane + jnp.where(row == 0, from_y_ref[c, x : x + 1, :], 0.0)

    corner = []
    for c in range(6):
        plane = with_y(edge_x_ref[c], c, nx)
        to_x_ref[c] = plane
        corner.append(plane)
    to_xz_ref[...] = lane_pick(jnp.concatenate(corner[:3] + [jnp.zeros((80, 128), jnp.float32)], axis=0), 127)
    for c in range(3):
        planes = [with_y(upper_ref[c, x], c, x) for x in range(nx)]
        to_z_ref[:, c * 128 : (c + 1) * 128] = lane_pick(jnp.concatenate(planes, axis=0), 127)


def pair_kernel(
    got_ref, got_rows_ref, own_ref, cent_ref, nodes_ref, upper_ref, lower_ref, from_y_ref, from_x_ref, from_z_ref,
    from_xz_ref, velocity_ref, disp_ref, mass_ref, velocity_out, disp_out, contact_ref, sums, targets, target_vec, slots, group_block, counts, features, middle_rows,
    near, semaphore,
):
    blocks = own_ref.shape[0]
    peers = got_ref.shape[0] // ROWS
    total_slots = peers * SLOTS
    target_rows = got_rows_ref[pl.ds(ROWS - 1, peers, stride=ROWS), :]
    if peers < 128:
        target_rows = jnp.concatenate([target_rows, jnp.full((128 - peers, 128), -1.0)], axis=0)
    target_rows = target_rows.T[0:8, :].astype(jnp.int32)
    lane = lax.broadcasted_iota(jnp.int32, (8, 128), 1)
    tally = jnp.zeros((8, 128), jnp.float32)
    for block in range(blocks):
        number = jnp.sum(jnp.where(target_rows == block, 1.0, 0.0), axis=1, keepdims=True)
        tally = jnp.where(lane == block, number, tally)
    target_vec[0:8, :] = target_rows
    target_vec[8:16, :] = tally.astype(jnp.int32)
    copy = pltpu.make_async_copy(target_vec, targets, semaphore)
    copy.start()
    sums[...] = jnp.zeros(sums.shape, jnp.float32)
    sub = lax.broadcasted_iota(jnp.int32, (8, FACETS), 0)
    far = jnp.where(sub == 3, -1.0e6, 0.0)
    features[total_slots] = jnp.concatenate([far, jnp.zeros((40, FACETS), jnp.float32)], axis=0).astype(jnp.bfloat16)
    for c in range(3):
        middle_rows[3 * total_slots + c] = jnp.zeros((1, FACETS), jnp.float32)
    copy.wait()
    place = 0
    for block in range(blocks):
        first = place
        for k in range(SLOTS):
            counts[k][block] = place
            place = place + targets[8 + k, block]
        for k in range(GROUP):
            slots[place + k] = total_slots
        place = (place + (GROUP - 1)) & ~(GROUP - 1)

        def name_groups(group, carry):
            group_block[group] = block
            return carry

        lax.fori_loop(first // GROUP, place // GROUP, name_groups, 0)
    for k in range(2 * AHEAD * GROUP):
        slots[place + k] = total_slots
    for k in range(2 * AHEAD):
        group_block[place // GROUP + k] = 0
    for k in range(SLOTS):
        counts[k][blocks] = unused_from(blocks, peers) + k * peers

    def prepare(peer, carry):
        for k in range(SLOTS):
            target = targets[k, peer]
            block = jnp.where(target < 0, blocks, target)
            spot = counts[k][block]
            counts[k][block] = spot + 1
            slots[spot] = peer * SLOTS + k
            x, y, z = [
                jnp.broadcast_to(got_ref[peer * ROWS + 3 * k + c], (8, FACETS)) - CENTER for c in range(3)
            ]
            away = x * x + y * y + z * z
            value = jnp.where(sub == 4, 1.0, -away)
            for index, part in enumerate((x, y, z)):
                middle_rows[3 * (peer * SLOTS + k) + index] = part[0:1]
                value = jnp.where(sub == index, part, value)
            value = jnp.where(sub > 4, 0.0, value)
            high, middle, low = split_3(value)
            features[peer * SLOTS + k] = jnp.concatenate(
                [high, middle, low, high, middle, high], axis=0
            ).astype(jnp.bfloat16)
        return carry

    lax.fori_loop(0, peers, prepare, 0, unroll=4)

    def reach(group, out):
        columns = [features[slots[group * GROUP + k]] for k in range(GROUP)]
        out[...] = jnp.dot(
            own_ref[group_block[group]][:, :48], jnp.concatenate(columns, axis=1), preferred_element_type=jnp.float32
        )

    def add(group, near):
        block = group_block[group]
        bases = [3 * slots[group * GROUP + k] for k in range(GROUP)]
        for start in range(0, FACETS, 16):
            part = slice(start, start + 16)
            total = [sums[block * 4 + q, part, :] for q in range(4)]
            for k in range(GROUP):
                weight = jnp.maximum(near[part, k * FACETS : (k + 1) * FACETS], 0.0)
                total[3] = total[3] + weight
                for c in range(3):
                    total[c] = total[c] + weight * middle_rows[bases[k] + c]
            for q in range(4):
                sums[block * 4 + q, part, :] = total[q]

    for i in range(AHEAD):
        reach(i, near[i])

    def some(step, carry):
        for i in range(AHEAD):
            add(step * AHEAD + i, near[i])
            reach((step + 1) * AHEAD + i, near[i])
        return carry

    lax.fori_loop(0, (place // GROUP + (AHEAD - 1)) // AHEAD, some, 0)
    scatter(sums, cent_ref, nodes_ref, contact_ref)
    update(
        contact_ref, upper_ref, lower_ref, from_y_ref, from_x_ref, from_z_ref, from_xz_ref, velocity_ref, disp_ref,
        mass_ref, velocity_out, disp_out,
    )


def unused_from(blocks, peers):
    return SLOTS * peers + (blocks + 2 * AHEAD) * GROUP


def pair_scratch(blocks, peers):
    return [
        pltpu.VMEM((384, 128), jnp.float32),
        pltpu.VMEM((blocks * 4, FACETS, FACETS), jnp.float32),
        pltpu.SMEM((16, 128), jnp.int32),
        pltpu.VMEM((16, 128), jnp.int32),
        pltpu.SMEM((unused_from(blocks, peers) + SLOTS * peers,), jnp.int32),
        pltpu.SMEM((SLOTS * peers // GROUP + blocks + 2 * AHEAD,), jnp.int32),
        [pltpu.SMEM((blocks + 1,), jnp.int32) for _ in range(SLOTS)],
        pltpu.VMEM((peers * SLOTS + 1, 48, FACETS), jnp.bfloat16),
        pltpu.VMEM((3 * peers * SLOTS + 3, 1, FACETS), jnp.float32),
        [pltpu.VMEM((FACETS, GROUP * FACETS), jnp.float32) for _ in range(AHEAD)],
        pltpu.SemaphoreType.DMA,
    ]


def scatter(sums_ref, cent_ref, nodes_ref, contact_ref):
    blocks = cent_ref.shape[0] // 3
    high_iota = lax.broadcasted_iota(jnp.int32, (64, FACETS), 0)
    low_iota = lax.broadcasted_iota(jnp.int32, (256, FACETS), 0)
    contact = jnp.zeros((192, 256), jnp.float32)
    for block in range(blocks):
        left, right = ([], [])
        total = [jnp.sum(sums_ref[block * 4 + q].T, axis=0, keepdims=True) for q in range(4)]
        parts = []
        for c in range(3):
            force = (cent_ref[block * 3 + c] - CENTER) * total[3] - total[c]
            high, rest = split_2(0.25 * PENALTY * force)
            parts.append((high.astype(jnp.float32), rest.astype(jnp.float32)))
        for m in range(4):
            ids = nodes_ref[block * 4 + m : block * 4 + m + 1, :]
            here = jnp.where(low_iota == (ids & 255), 1.0, 0.0).astype(jnp.bfloat16)
            in_row = high_iota == (ids >> 8)
            for part in range(2):
                left.append(
                    jnp.concatenate(
                        [jnp.where(in_row, parts[c][part], 0.0).astype(jnp.bfloat16) for c in range(3)], axis=0
                    )
                )
                right.append(here)
        contact = contact + lax.dot_general(
            jnp.concatenate(left, axis=1), jnp.concatenate(right, axis=1), NT, preferred_element_type=jnp.float32
        )
    contact_ref[pl.ds(0, 192, stride=2), :] = contact[:, :128]
    contact_ref[pl.ds(1, 192, stride=2), :] = contact[:, 128:]


def update(
    contact, upper_ref, lower_ref, from_y_ref, from_x_ref, from_z_ref, from_xz_ref, velocity_ref, disp_ref,
    mass_ref, velocity_out, disp_out,
):
    nx = velocity_ref.shape[1]
    columns = columns_of(jnp.concatenate(rows_of(from_z_ref[...]) + [from_xz_ref[...]], axis=0))
    lane = lax.broadcasted_iota(jnp.int32, (16, 128), 1)
    row = lax.broadcasted_iota(jnp.int32, (16, 128), 0)
    for c in range(3):
        for x in range(nx):
            upper = upper_ref[c, x] + jnp.where(row == 0, from_y_ref[c, x : x + 1, :], 0.0)
            lower = lower_ref[c, x] + jnp.where(row == 0, from_y_ref[3 + c, x : x + 1, :], 0.0)
            below = columns[x * 16 : x * 16 + 16, c : c + 1]
            if x == 0:
                upper = upper + from_x_ref[c]
                lower = lower + from_x_ref[3 + c]
                below = below + columns[c * 16 : c * 16 + 16, 3:4]
            internal = lower + jnp.where(lane == 0, below, pltpu.roll(upper, 1, 1))
            force = contact[c * 128 + x * 16 : c * 128 + x * 16 + 16, :]
            velocity = velocity_ref[c, x] + TIME_STEP * (force - internal) / mass_ref[x]
            velocity_out[c, x] = velocity
            disp_out[c, x] = disp_ref[c, x] + TIME_STEP * velocity


def shifted(value, axis, step):
    count = lax.axis_size(axis)
    return lax.ppermute(value, axis, [(i, i + step) for i in range(count) if 0 <= i + step < count])


def shifted_xz(value, step):
    count_x, count_z = lax.axis_size("gx"), lax.axis_size("gz")
    pairs = [
        (i * count_z + j, (i + step) * count_z + j + step)
        for i in range(count_x)
        for j in range(count_z)
        if 0 <= i + step < count_x and 0 <= j + step < count_z
    ]
    return lax.ppermute(value, ("gx", "gz"), pairs)


def f32(*shape):
    return jax.ShapeDtypeStruct(shape, jnp.float32)


def on_device(
    velocity,
    displacement,
    mass,
    stress,
    plastic,
    yield_stress,
    facet_anchor,
    facet_nodes,
    pair_source,
    pair_dest,
    pair_target,
):
    size_x, size_y, size_z = velocity.shape[1:]
    blocks = facet_anchor.shape[3]
    pairs = pair_source.shape[3]
    peers = lax.axis_size("gx") * lax.axis_size("gz")
    flat_disp = displacement.reshape(-1, size_z)
    nodes = facet_nodes.reshape(blocks * 4, FACETS)
    anchors = facet_anchor.reshape(blocks, 3, FACETS).transpose(1, 0, 2).reshape(3 * blocks, FACETS)
    barrier = lax.optimization_barrier

    low_z, low_x, low_y = pl.pallas_call(
        faces_kernel, out_shape=(f32(1, 384), f32(48, size_z), f32(24, size_z)), compiler_params=params(8), name="faces"
    )(velocity)
    centroids, send = pl.pallas_call(
        begin_kernel,
        out_shape=(
            f32(blocks * 3, 1, FACETS),
            f32(peers * ROWS, 1, FACETS),
        ),
        in_specs=[VMEM, VMEM, VMEM, HBM, HBM, HBM],
        scratch_shapes=[
            pltpu.SMEM((pairs,), jnp.int32),
            pltpu.SMEM((pairs,), jnp.int32),
            pltpu.SMEM((pairs,), jnp.int32),
            pltpu.SMEM((peers,), jnp.int32),
            pltpu.SMEM((peers * SLOTS,), jnp.int32),
            pltpu.SemaphoreType.DMA((3,)),
        ],
        compiler_params=pltpu.CompilerParams(vmem_limit_bytes=64 * 1024 * 1024 - 128 * 1024),
        name="begin",
    )(
        flat_disp,
        anchors,
        nodes,
        pair_source.reshape(pairs),
        pair_dest.reshape(pairs),
        pair_target.reshape(pairs),
    )
    face_z = shifted(low_z, "gz", -1)
    face_x = shifted(low_x, "gx", -1)
    face_xz = shifted_xz(low_z, -1)
    send, face_x, face_z, face_xz = barrier((send, face_x, face_z, face_xz))
    got = lax.all_to_all(send, ("gx", "gz"), split_axis=0, concat_axis=0, tiled=True)
    edges = pl.pallas_call(edges_kernel, out_shape=f32(40, size_z), compiler_params=params(8), name="edges")(
        low_y, face_x, face_z, face_xz
    )
    face_y = shifted(edges, "gy", -1)
    own = pl.pallas_call(
        own_kernel,
        out_shape=jax.ShapeDtypeStruct((blocks, FACETS, 128), jnp.bfloat16),
        compiler_params=params(8),
        name="own",
    )(centroids)
    stress_new, plastic_new, upper, lower, edge_y, edge_x = pl.pallas_call(
        stress_kernel,
        out_shape=(
            f32(*stress.shape),
            f32(*plastic.shape),
            f32(*velocity.shape),
            f32(*velocity.shape),
            f32(6, size_x + 1, size_z),
            f32(6, size_y, size_z),
        ),
        compiler_params=params(16),
        name="stress",
    )(velocity, face_z, face_x, face_xz, face_y, stress, plastic, yield_stress)
    from_y = shifted(edge_y, "gy", 1)
    to_x, to_z, to_xz = pl.pallas_call(
        force_kernel,
        out_shape=(f32(6, size_y, size_z), f32(1, 384), f32(1, 128)),
        compiler_params=params(8),
        name="force",
    )(upper, edge_x, from_y)
    from_x = shifted(to_x, "gx", 1)
    from_z = shifted(to_z, "gz", 1)
    from_xz = shifted_xz(to_xz, 1)
    velocity_new, displacement_new = pl.pallas_call(
        pair_kernel,
        out_shape=(f32(*velocity.shape), f32(*velocity.shape)),
        scratch_shapes=pair_scratch(blocks, peers),
        compiler_params=params(24),
        name="pairs",
    )(
        got,
        got.reshape(peers * ROWS, FACETS),
        own,
        centroids,
        nodes,
        upper,
        lower,
        from_y,
        from_x,
        from_z,
        from_xz,
        velocity,
        displacement,
        mass,
    )
    return (velocity_new, displacement_new, stress_new, plastic_new)


def solution(mesh):
    return jax.shard_map(
        on_device,
        mesh=mesh,
        in_specs=(
            P(None, "gx", "gy", "gz"),
            P(None, "gx", "gy", "gz"),
            P("gx", "gy", "gz"),
            P(None, "gx", "gy", "gz"),
            P("gx", "gy", "gz"),
            P("gx", "gy", "gz"),
            P("gx", "gy", "gz", None, None, None),
            P("gx", "gy", "gz", None, None, None),
            P("gx", "gy", "gz", None),
            P("gx", "gy", "gz", None, None),
            P("gx", "gy", "gz", None),
        ),
        out_specs=(
            P(None, "gx", "gy", "gz"),
            P(None, "gx", "gy", "gz"),
            P(None, "gx", "gy", "gz"),
            P("gx", "gy", "gz"),
        ),
        check_vma=False,
    )
```

```python
import jax
import jax.numpy as jnp
from jax import lax
from jax.experimental import pallas as pl
from jax.experimental.pallas import tpu as pltpu
from jax.sharding import PartitionSpec as P

FACETS = 128
SLOTS = 4
CENTER = 2.0
GROUP = 8
AHEAD = 4
ROWS = 13
TIME_STEP = 0.25
SHEAR_MODULUS = 1.0
BULK_MODULUS = 2.0
HARDENING = 1.0
PENALTY = 1.0
REACH_SQUARED = 1.0
VOIGT = ((0, 3, 5), (3, 1, 4), (5, 4, 2))
NT = (((1,), (1,)), ((), ()))
VMEM = pl.BlockSpec(memory_space=pltpu.VMEM)
HBM = pl.BlockSpec(memory_space=pltpu.HBM)


def params(mib):
    return pltpu.CompilerParams(vmem_limit_bytes=mib * 1024 * 1024)


def split_2(value):
    high = value.astype(jnp.bfloat16)
    rest = (value - high.astype(jnp.float32)).astype(jnp.bfloat16)
    return high, rest


def lane_pick(value, lane):
    pick = (lax.broadcasted_iota(jnp.int32, (8, 128), 1) == lane).astype(jnp.float32)
    return lax.dot_general(
        pick, value, NT, precision=lax.Precision.HIGHEST, preferred_element_type=jnp.float32
    )[0:1]


def columns_of(rows):
    count = rows.shape[0]
    padded = jnp.concatenate([rows, jnp.zeros((128 - count, 128), jnp.float32)], axis=0)
    return padded.T


def rows_of(row):
    return [row[:, c * 128 : (c + 1) * 128] for c in range(row.shape[1] // 128)]


def edges_kernel(low_y_ref, face_x_ref, face_z_ref, face_xz_ref, out_ref):
    rows = [face_x_ref[c * 16 : c * 16 + 1, :] for c in range(3)]
    rows = rows + rows_of(face_z_ref[...]) + rows_of(face_xz_ref[...])
    out_ref[...] = jnp.concatenate([low_y_ref[...]] + rows + [jnp.zeros((7, 128), jnp.float32)], axis=0)


def faces_kernel(
    velocity_ref, disp_ref, anchor_ref, nodes_ref, low_z_ref, low_x_ref, low_y_ref, cent_ref
):
    for c in range(3):
        planes = [velocity_ref[c, x] for x in range(velocity_ref.shape[1])]
        low_z_ref[:, c * 128 : (c + 1) * 128] = lane_pick(jnp.concatenate(planes, axis=0), 0)
        low_x_ref[c * 16 : (c + 1) * 16, :] = planes[0]
        low_y_ref[c * 8 : (c + 1) * 8, :] = jnp.concatenate([plane[0:1] for plane in planes], axis=0)
    high, rest = split_2(disp_ref[...])
    table = jnp.concatenate([high, rest], axis=1)
    iota = lax.broadcasted_iota(jnp.int32, (128, 4 * FACETS), 0)
    blocks = anchor_ref.shape[0] // 3
    for block in range(blocks):
        ids = jnp.concatenate([nodes_ref[block * 4 + m : block * 4 + m + 1, :] for m in range(4)], axis=1)
        here = jnp.where(iota == (ids & 127), 1.0, 0.0).astype(jnp.bfloat16)
        picked = jnp.dot(table, jnp.concatenate([here, here], axis=0), preferred_element_type=jnp.float32)
        in_row = iota == (ids >> 7)
        for c in range(3):
            kept = jnp.where(in_row, picked[c * 128 : (c + 1) * 128], 0.0)
            total = kept[:, :128] + kept[:, 128:256] + kept[:, 256:384] + kept[:, 384:]
            total = jnp.sum(total, axis=0, keepdims=True)
            cent_ref[block * 3 + c] = anchor_ref[c * blocks + block : c * blocks + block + 1, :] + 0.25 * total


def begin_kernel(
    cent_ref, source_hbm, dest_hbm, target_hbm, send_ref, source_ref, dest_ref, target_ref, count, slot_target, sems,
):
    peers = send_ref.shape[0] // ROWS
    pairs = source_ref.shape[0]
    copies = [
        pltpu.make_async_copy(source_hbm, source_ref, sems.at[0]),
        pltpu.make_async_copy(dest_hbm, dest_ref, sems.at[1]),
        pltpu.make_async_copy(target_hbm, target_ref, sems.at[2]),
    ]
    for copy in copies:
        copy.start()
    for peer in range(peers):
        count[peer] = 0
    for slot in range(peers * SLOTS):
        slot_target[slot] = -1
    for copy in copies:
        copy.wait()

    def place(pair, carry):
        dest = dest_ref[pair]
        slot = count[dest]
        count[dest] = slot + 1
        slot_target[dest * SLOTS + slot] = target_ref[pair]
        send_ref[pl.ds(dest * ROWS + 3 * slot, 3)] = cent_ref[pl.ds(source_ref[pair] * 3, 3)]
        return carry

    lax.fori_loop(0, pairs, place, 0, unroll=8)
    lane = lax.broadcasted_iota(jnp.int32, (1, 128), 1)

    def write_targets(peer, carry):
        row = jnp.full((1, 128), -1, jnp.int32)
        for k in range(SLOTS):
            row = jnp.where(lane == k, slot_target[peer * SLOTS + k], row)
        send_ref[peer * ROWS + ROWS - 1] = row.astype(jnp.float32)
        return carry

    lax.fori_loop(0, peers, write_targets, 0, unroll=8)


def split_3(value):
    high = value.astype(jnp.bfloat16).astype(jnp.float32)
    rest = value - high
    middle = rest.astype(jnp.bfloat16).astype(jnp.float32)
    return high, middle, rest - middle


def own_kernel(cent_ref, own_ref):
    for block in range(own_ref.shape[0]):
        x, y, z = [cent_ref[block * 3 + c] - CENTER for c in range(3)]
        one = jnp.ones_like(x)
        rows = [2.0 * x, 2.0 * y, 2.0 * z, one, REACH_SQUARED - (x * x + y * y + z * z)]
        features = jnp.concatenate(rows + [jnp.zeros((3, FACETS), jnp.float32)], axis=0)
        high, middle, low = split_3(features)
        parts = jnp.concatenate([high, high, high, middle, middle, low, jnp.zeros((80, FACETS), jnp.float32)], axis=0)
        own_ref[block] = parts.T.astype(jnp.bfloat16)


def stress_kernel(
    velocity_ref, face_z_ref, face_x_ref, face_xz_ref, face_y_ref, stress_ref, plastic_ref, yield_ref,
    stress_out, plastic_out, upper_out, lower_out, edge_y_out, edge_x_out,
):
    nx = velocity_ref.shape[1]
    columns = columns_of(
        jnp.concatenate(rows_of(face_z_ref[...]) + rows_of(face_xz_ref[...]) + [face_y_ref[27:33, :]], axis=0)
    )
    lane = lax.broadcasted_iota(jnp.int32, (16, 128), 1)
    row = lax.broadcasted_iota(jnp.int32, (16, 128), 0)
    grad_x, grad_y, grad_z = ([], [], [])
    for c in range(3):
        sum_yz, dif_y, dif_z = ([], [], [])
        for x in range(nx + 1):
            if x < nx:
                plane = velocity_ref[c, x]
                beyond = columns[x * 16 : x * 16 + 16, c : c + 1]
                edge = face_y_ref[c * 8 + x : c * 8 + x + 1, :]
                edge_beyond = columns[x * 16 : x * 16 + 1, 6 + c : 7 + c]
            else:
                plane = face_x_ref[c * 16 : c * 16 + 16, :]
                beyond = columns[0:16, 3 + c : 4 + c]
                edge = face_y_ref[24 + c : 25 + c, :]
                edge_beyond = columns[0:1, 9 + c : 10 + c]
            edge = jnp.broadcast_to(edge, (16, 128))
            after = jnp.where(lane == 127, beyond, pltpu.roll(plane, 127, 1))
            edge_after = jnp.where(lane == 127, edge_beyond, pltpu.roll(edge, 127, 1))
            sum_z, dif = plane + after, after - plane
            sum_z_next = jnp.where(row == 15, edge + edge_after, pltpu.roll(sum_z, 15, 0))
            dif_next = jnp.where(row == 15, edge_after - edge, pltpu.roll(dif, 15, 0))
            sum_yz.append(sum_z + sum_z_next)
            dif_y.append(sum_z_next - sum_z)
            dif_z.append(dif + dif_next)
        grad_x.append([0.25 * (sum_yz[x + 1] - sum_yz[x]) for x in range(nx)])
        grad_y.append([0.25 * (dif_y[x + 1] + dif_y[x]) for x in range(nx)])
        grad_z.append([0.25 * (dif_z[x + 1] + dif_z[x]) for x in range(nx)])
    stresses = []
    for x in range(nx):
        inc = [TIME_STEP * grad_x[0][x], TIME_STEP * grad_y[1][x], TIME_STEP * grad_z[2][x]]
        shear = [
            TIME_STEP * 0.5 * (grad_y[0][x] + grad_x[1][x]),
            TIME_STEP * 0.5 * (grad_z[1][x] + grad_y[2][x]),
            TIME_STEP * 0.5 * (grad_z[0][x] + grad_x[2][x]),
        ]
        volume = inc[0] + inc[1] + inc[2]
        trial = [
            stress_ref[d, x] + 2.0 * SHEAR_MODULUS * (inc[d] - volume / 3.0) + BULK_MODULUS * volume
            for d in range(3)
        ]
        trial_shear = [stress_ref[3 + d, x] + 2.0 * SHEAR_MODULUS * shear[d] for d in range(3)]
        mean = (trial[0] + trial[1] + trial[2]) / 3.0
        dev = [trial[d] - mean for d in range(3)]
        square = dev[0] * dev[0] + dev[1] * dev[1] + dev[2] * dev[2]
        square = square + 2.0 * (
            trial_shear[0] * trial_shear[0] + trial_shear[1] * trial_shear[1] + trial_shear[2] * trial_shear[2]
        )
        equivalent = jnp.sqrt(1.5 * square)
        plastic = plastic_ref[x]
        limit = yield_ref[x] + HARDENING * plastic
        gamma = jnp.maximum(equivalent - limit, 0.0) / (3.0 * SHEAR_MODULUS + HARDENING)
        factor = 1.0 - 3.0 * SHEAR_MODULUS * gamma / jnp.maximum(equivalent, limit)
        new = [dev[d] * factor + mean for d in range(3)] + [trial_shear[d] * factor for d in range(3)]
        for d in range(6):
            stress_out[d, x] = new[d]
        plastic_out[x] = plastic + gamma
        stresses.append(new)
    for c in range(3):
        before = None
        edge_before = None
        for x in range(nx + 1):
            if x < nx:
                s = [0.25 * stresses[x][VOIGT[c][d]] for d in range(3)]
                down = [jnp.where(row == 0, 0.0, pltpu.roll(v, 1, 0)) for v in s]
                here = [down[0] + s[0], down[1] - s[1], down[2] + s[2]]
                edge_here = [v[15:16] for v in s]
            if x == 0:
                x0, x1, x2 = -here[0], here[1], here[2]
                e0, e1, e2 = -edge_here[0], edge_here[1], edge_here[2]
            elif x < nx:
                x0, x1, x2 = before[0] - here[0], before[1] + here[1], before[2] + here[2]
                e0, e1, e2 = (
                    edge_before[0] - edge_here[0], edge_before[1] + edge_here[1], edge_before[2] + edge_here[2]
                )
            else:
                x0, x1, x2 = before
                e0, e1, e2 = edge_before
            both = x0 + x1
            edge_both = e0 + e1
            if x < nx:
                upper_out[c, x] = both + x2
                lower_out[c, x] = both - x2
            else:
                edge_x_out[c] = both + x2
                edge_x_out[3 + c] = both - x2
            edge_y_out[c, x : x + 1, :] = edge_both + e2
            edge_y_out[3 + c, x : x + 1, :] = edge_both - e2
            before, edge_before = here, edge_here


def force_kernel(upper_ref, edge_x_ref, from_y_ref, to_x_ref, to_z_ref, to_xz_ref):
    nx = upper_ref.shape[1]
    row = lax.broadcasted_iota(jnp.int32, (16, 128), 0)

    def with_y(plane, c, x):
        return plane + jnp.where(row == 0, from_y_ref[c, x : x + 1, :], 0.0)

    corner = []
    for c in range(6):
        plane = with_y(edge_x_ref[c], c, nx)
        to_x_ref[c] = plane
        corner.append(plane)
    to_xz_ref[...] = lane_pick(jnp.concatenate(corner[:3] + [jnp.zeros((80, 128), jnp.float32)], axis=0), 127)
    for c in range(3):
        planes = [with_y(upper_ref[c, x], c, x) for x in range(nx)]
        to_z_ref[:, c * 128 : (c + 1) * 128] = lane_pick(jnp.concatenate(planes, axis=0), 127)


def pair_kernel(
    got_ref, got_rows_ref, own_ref, cent_ref, nodes_ref, upper_ref, lower_ref, from_y_ref, from_x_ref, from_z_ref,
    from_xz_ref, velocity_ref, disp_ref, mass_ref, velocity_out, disp_out, contact_ref, sums, targets, target_vec, slots, group_block, counts, features, middle_rows,
    near, semaphore,
):
    blocks = own_ref.shape[0]
    peers = got_ref.shape[0] // ROWS
    total_slots = peers * SLOTS
    target_rows = got_rows_ref[pl.ds(ROWS - 1, peers, stride=ROWS), :]
    if peers < 128:
        target_rows = jnp.concatenate([target_rows, jnp.full((128 - peers, 128), -1.0)], axis=0)
    target_rows = target_rows.T[0:8, :].astype(jnp.int32)
    lane = lax.broadcasted_iota(jnp.int32, (8, 128), 1)
    tally = jnp.zeros((8, 128), jnp.float32)
    for block in range(blocks):
        number = jnp.sum(jnp.where(target_rows == block, 1.0, 0.0), axis=1, keepdims=True)
        tally = jnp.where(lane == block, number, tally)
    target_vec[0:8, :] = target_rows
    target_vec[8:16, :] = tally.astype(jnp.int32)
    copy = pltpu.make_async_copy(target_vec, targets, semaphore)
    copy.start()
    sums[...] = jnp.zeros(sums.shape, jnp.float32)
    sub = lax.broadcasted_iota(jnp.int32, (8, FACETS), 0)
    far = jnp.where(sub == 3, -1.0e6, 0.0)
    features[total_slots] = jnp.concatenate([far, jnp.zeros((40, FACETS), jnp.float32)], axis=0).astype(jnp.bfloat16)
    for c in range(3):
        middle_rows[3 * total_slots + c] = jnp.zeros((1, FACETS), jnp.float32)
    copy.wait()
    place = 0
    for block in range(blocks):
        first = place
        for k in range(SLOTS):
            counts[k][block] = place
            place = place + targets[8 + k, block]
        for k in range(GROUP):
            slots[place + k] = total_slots
        place = (place + (GROUP - 1)) & ~(GROUP - 1)

        def name_groups(group, carry):
            group_block[group] = block
            return carry

        lax.fori_loop(first // GROUP, place // GROUP, name_groups, 0)
    for k in range(2 * AHEAD * GROUP):
        slots[place + k] = total_slots
    for k in range(2 * AHEAD):
        group_block[place // GROUP + k] = 0
    for k in range(SLOTS):
        counts[k][blocks] = unused_from(blocks, peers) + k * peers

    def prepare(peer, carry):
        for k in range(SLOTS):
            target = targets[k, peer]
            block = jnp.where(target < 0, blocks, target)
            spot = counts[k][block]
            counts[k][block] = spot + 1
            slots[spot] = peer * SLOTS + k
            x, y, z = [
                jnp.broadcast_to(got_ref[peer * ROWS + 3 * k + c], (8, FACETS)) - CENTER for c in range(3)
            ]
            away = x * x + y * y + z * z
            value = jnp.where(sub == 4, 1.0, -away)
            for index, part in enumerate((x, y, z)):
                middle_rows[3 * (peer * SLOTS + k) + index] = part[0:1]
                value = jnp.where(sub == index, part, value)
            value = jnp.where(sub > 4, 0.0, value)
            high, middle, low = split_3(value)
            features[peer * SLOTS + k] = jnp.concatenate(
                [high, middle, low, high, middle, high], axis=0
            ).astype(jnp.bfloat16)
        return carry

    lax.fori_loop(0, peers, prepare, 0, unroll=4)

    def reach(group, out):
        columns = [features[slots[group * GROUP + k]] for k in range(GROUP)]
        out[...] = jnp.dot(
            own_ref[group_block[group]][:, :48], jnp.concatenate(columns, axis=1), preferred_element_type=jnp.float32
        )

    def add(group, near):
        block = group_block[group]
        bases = [3 * slots[group * GROUP + k] for k in range(GROUP)]
        for start in range(0, FACETS, 16):
            part = slice(start, start + 16)
            total = [sums[block * 4 + q, part, :] for q in range(4)]
            for k in range(GROUP):
                weight = jnp.maximum(near[part, k * FACETS : (k + 1) * FACETS], 0.0)
                total[3] = total[3] + weight
                for c in range(3):
                    total[c] = total[c] + weight * middle_rows[bases[k] + c]
            for q in range(4):
                sums[block * 4 + q, part, :] = total[q]

    for i in range(AHEAD):
        reach(i, near[i])

    def some(step, carry):
        for i in range(AHEAD):
            add(step * AHEAD + i, near[i])
            reach((step + 1) * AHEAD + i, near[i])
        return carry

    lax.fori_loop(0, (place // GROUP + (AHEAD - 1)) // AHEAD, some, 0)
    scatter(sums, cent_ref, nodes_ref, contact_ref)
    update(
        contact_ref, upper_ref, lower_ref, from_y_ref, from_x_ref, from_z_ref, from_xz_ref, velocity_ref, disp_ref,
        mass_ref, velocity_out, disp_out,
    )


def unused_from(blocks, peers):
    return SLOTS * peers + (blocks + 2 * AHEAD) * GROUP


def pair_scratch(blocks, peers):
    return [
        pltpu.VMEM((384, 128), jnp.float32),
        pltpu.VMEM((blocks * 4, FACETS, FACETS), jnp.float32),
        pltpu.SMEM((16, 128), jnp.int32),
        pltpu.VMEM((16, 128), jnp.int32),
        pltpu.SMEM((unused_from(blocks, peers) + SLOTS * peers,), jnp.int32),
        pltpu.SMEM((SLOTS * peers // GROUP + blocks + 2 * AHEAD,), jnp.int32),
        [pltpu.SMEM((blocks + 1,), jnp.int32) for _ in range(SLOTS)],
        pltpu.VMEM((peers * SLOTS + 1, 48, FACETS), jnp.bfloat16),
        pltpu.VMEM((3 * peers * SLOTS + 3, 1, FACETS), jnp.float32),
        [pltpu.VMEM((FACETS, GROUP * FACETS), jnp.float32) for _ in range(AHEAD)],
        pltpu.SemaphoreType.DMA,
    ]


def scatter(sums_ref, cent_ref, nodes_ref, contact_ref):
    blocks = cent_ref.shape[0] // 3
    high_iota = lax.broadcasted_iota(jnp.int32, (64, FACETS), 0)
    low_iota = lax.broadcasted_iota(jnp.int32, (256, FACETS), 0)
    contact = jnp.zeros((192, 256), jnp.float32)
    for block in range(blocks):
        left, right = ([], [])
        total = [jnp.sum(sums_ref[block * 4 + q].T, axis=0, keepdims=True) for q in range(4)]
        parts = []
        for c in range(3):
            force = (cent_ref[block * 3 + c] - CENTER) * total[3] - total[c]
            high, rest = split_2(0.25 * PENALTY * force)
            parts.append((high.astype(jnp.float32), rest.astype(jnp.float32)))
        for m in range(4):
            ids = nodes_ref[block * 4 + m : block * 4 + m + 1, :]
            here = jnp.where(low_iota == (ids & 255), 1.0, 0.0).astype(jnp.bfloat16)
            in_row = high_iota == (ids >> 8)
            for part in range(2):
                left.append(
                    jnp.concatenate(
                        [jnp.where(in_row, parts[c][part], 0.0).astype(jnp.bfloat16) for c in range(3)], axis=0
                    )
                )
                right.append(here)
        contact = contact + lax.dot_general(
            jnp.concatenate(left, axis=1), jnp.concatenate(right, axis=1), NT, preferred_element_type=jnp.float32
        )
    contact_ref[pl.ds(0, 192, stride=2), :] = contact[:, :128]
    contact_ref[pl.ds(1, 192, stride=2), :] = contact[:, 128:]


def update(
    contact, upper_ref, lower_ref, from_y_ref, from_x_ref, from_z_ref, from_xz_ref, velocity_ref, disp_ref,
    mass_ref, velocity_out, disp_out,
):
    nx = velocity_ref.shape[1]
    columns = columns_of(jnp.concatenate(rows_of(from_z_ref[...]) + [from_xz_ref[...]], axis=0))
    lane = lax.broadcasted_iota(jnp.int32, (16, 128), 1)
    row = lax.broadcasted_iota(jnp.int32, (16, 128), 0)
    for c in range(3):
        for x in range(nx):
            upper = upper_ref[c, x] + jnp.where(row == 0, from_y_ref[c, x : x + 1, :], 0.0)
            lower = lower_ref[c, x] + jnp.where(row == 0, from_y_ref[3 + c, x : x + 1, :], 0.0)
            below = columns[x * 16 : x * 16 + 16, c : c + 1]
            if x == 0:
                upper = upper + from_x_ref[c]
                lower = lower + from_x_ref[3 + c]
                below = below + columns[c * 16 : c * 16 + 16, 3:4]
            internal = lower + jnp.where(lane == 0, below, pltpu.roll(upper, 1, 1))
            force = contact[c * 128 + x * 16 : c * 128 + x * 16 + 16, :]
            velocity = velocity_ref[c, x] + TIME_STEP * (force - internal) / mass_ref[x]
            velocity_out[c, x] = velocity
            disp_out[c, x] = disp_ref[c, x] + TIME_STEP * velocity


def shifted(value, axis, step):
    count = lax.axis_size(axis)
    return lax.ppermute(value, axis, [(i, i + step) for i in range(count) if 0 <= i + step < count])


def shifted_xz(value, step):
    count_x, count_z = lax.axis_size("gx"), lax.axis_size("gz")
    pairs = [
        (i * count_z + j, (i + step) * count_z + j + step)
        for i in range(count_x)
        for j in range(count_z)
        if 0 <= i + step < count_x and 0 <= j + step < count_z
    ]
    return lax.ppermute(value, ("gx", "gz"), pairs)


def f32(*shape):
    return jax.ShapeDtypeStruct(shape, jnp.float32)


def on_device(
    velocity,
    displacement,
    mass,
    stress,
    plastic,
    yield_stress,
    facet_anchor,
    facet_nodes,
    pair_source,
    pair_dest,
    pair_target,
):
    size_x, size_y, size_z = velocity.shape[1:]
    blocks = facet_anchor.shape[3]
    pairs = pair_source.shape[3]
    peers = lax.axis_size("gx") * lax.axis_size("gz")
    flat_disp = displacement.reshape(-1, size_z)
    nodes = facet_nodes.reshape(blocks * 4, FACETS)
    anchors = facet_anchor.reshape(blocks, 3, FACETS).transpose(1, 0, 2).reshape(3 * blocks, FACETS)
    barrier = lax.optimization_barrier

    whole = pltpu.CompilerParams(vmem_limit_bytes=64 * 1024 * 1024 - 128 * 1024)
    low_z, low_x, low_y, centroids = pl.pallas_call(
        faces_kernel,
        out_shape=(f32(1, 384), f32(48, size_z), f32(24, size_z), f32(blocks * 3, 1, FACETS)),
        compiler_params=whole,
        name="faces",
    )(velocity, flat_disp, anchors, nodes)
    send = pl.pallas_call(
        begin_kernel,
        out_shape=f32(peers * ROWS, 1, FACETS),
        in_specs=[VMEM, HBM, HBM, HBM],
        scratch_shapes=[
            pltpu.SMEM((pairs,), jnp.int32),
            pltpu.SMEM((pairs,), jnp.int32),
            pltpu.SMEM((pairs,), jnp.int32),
            pltpu.SMEM((peers,), jnp.int32),
            pltpu.SMEM((peers * SLOTS,), jnp.int32),
            pltpu.SemaphoreType.DMA((3,)),
        ],
        compiler_params=whole,
        name="begin",
    )(
        centroids,
        pair_source.reshape(pairs),
        pair_dest.reshape(pairs),
        pair_target.reshape(pairs),
    )
    face_z = shifted(low_z, "gz", -1)
    face_x = shifted(low_x, "gx", -1)
    face_xz = shifted_xz(low_z, -1)
    send, face_x, face_z, face_xz = barrier((send, face_x, face_z, face_xz))
    got = lax.all_to_all(send, ("gx", "gz"), split_axis=0, concat_axis=0, tiled=True)
    edges = pl.pallas_call(edges_kernel, out_shape=f32(40, size_z), compiler_params=params(8), name="edges")(
        low_y, face_x, face_z, face_xz
    )
    face_y = shifted(edges, "gy", -1)
    own = pl.pallas_call(
        own_kernel,
        out_shape=jax.ShapeDtypeStruct((blocks, FACETS, 128), jnp.bfloat16),
        compiler_params=params(8),
        name="own",
    )(centroids)
    stress_new, plastic_new, upper, lower, edge_y, edge_x = pl.pallas_call(
        stress_kernel,
        out_shape=(
            f32(*stress.shape),
            f32(*plastic.shape),
            f32(*velocity.shape),
            f32(*velocity.shape),
            f32(6, size_x + 1, size_z),
            f32(6, size_y, size_z),
        ),
        compiler_params=params(16),
        name="stress",
    )(velocity, face_z, face_x, face_xz, face_y, stress, plastic, yield_stress)
    from_y = shifted(edge_y, "gy", 1)
    to_x, to_z, to_xz = pl.pallas_call(
        force_kernel,
        out_shape=(f32(6, size_y, size_z), f32(1, 384), f32(1, 128)),
        compiler_params=params(8),
        name="force",
    )(upper, edge_x, from_y)
    from_x = shifted(to_x, "gx", 1)
    from_z = shifted(to_z, "gz", 1)
    from_xz = shifted_xz(to_xz, 1)
    velocity_new, displacement_new = pl.pallas_call(
        pair_kernel,
        out_shape=(f32(*velocity.shape), f32(*velocity.shape)),
        scratch_shapes=pair_scratch(blocks, peers),
        compiler_params=params(24),
        name="pairs",
    )(
        got,
        got.reshape(peers * ROWS, FACETS),
        own,
        centroids,
        nodes,
        upper,
        lower,
        from_y,
        from_x,
        from_z,
        from_xz,
        velocity,
        displacement,
        mass,
    )
    return (velocity_new, displacement_new, stress_new, plastic_new)


def solution(mesh):
    return jax.shard_map(
        on_device,
        mesh=mesh,
        in_specs=(
            P(None, "gx", "gy", "gz"),
            P(None, "gx", "gy", "gz"),
            P("gx", "gy", "gz"),
            P(None, "gx", "gy", "gz"),
            P("gx", "gy", "gz"),
            P("gx", "gy", "gz"),
            P("gx", "gy", "gz", None, None, None),
            P("gx", "gy", "gz", None, None, None),
            P("gx", "gy", "gz", None),
            P("gx", "gy", "gz", None, None),
            P("gx", "gy", "gz", None),
        ),
        out_specs=(
            P(None, "gx", "gy", "gz"),
            P(None, "gx", "gy", "gz"),
            P(None, "gx", "gy", "gz"),
            P("gx", "gy", "gz"),
        ),
        check_vma=False,
    )
```
